512 devices in a mesh: seq: 8 (over x, core), exp: 64 (over y, z).
Axes of the slice: x: 4, y: 8, z: 8, core: 2. Of those that a mesh axis runs over, the one named last changes fastest.
Arguments:
- hidden: bfloat16 [65536, 1024], P(('seq', 'exp')), may hold values from -6 to 6
- queries: bfloat16 [65536, 1024], P(('seq', 'exp')), may hold values from -16 to 16
- thinker_keys: bfloat16 [4096, 128], P(('seq', 'exp')), may hold values from -16 to 16
- thinker_values: bfloat16 [4096, 128], P(('seq', 'exp')), may hold values from -15 to 15
- thinker_lengths: int32 [2048], P(('seq', 'exp')), may hold values from 1 to 8, 4096 in all
- out_proj: bfloat16 [1024, 1024], replicated, may hold values from -0.1875 to 0.1875
- expert_ids: int32 [65536, 4], P(('seq', 'exp')), may hold values from 0 to 63, all different within a row; in each aligned block of 128 rows (0 to 127, 128 to 255, ...) at most 10 rows name the same one
- gate_values: bfloat16 [65536, 4], P(('seq', 'exp')), may hold values from 0.099609375 to 1
- w_gate: bfloat16 [64, 1024, 768], P('exp', 'seq'), may hold values from -0.1875 to 0.1875
- w_up: bfloat16 [64, 1024, 768], P('exp', 'seq'), may hold values from -0.1875 to 0.1875
- w_down: bfloat16 [64, 768, 1024], P('exp', None, 'seq'), may hold values from -0.21875 to 0.21875
- cotangent: bfloat16 [65536, 1024], P(('seq', 'exp')), may hold values from -2.5 to 2.5
Outputs:
- grad_input: float32 [65536, 1024], P(('seq', 'exp'))
- grad_gates: bfloat16 [65536, 4], P(('seq', 'exp'))
The draws below stay inside these ranges and needn't reach their ends.
Inputs may be any that keep to these rules, and one draw needn't show every extreme that they name: `thinker_lengths`: each talker group of 32 tokens brings at least one thinker row, the groups of the dialogue together bring 4096, and some group brings exactly 8. `expert_ids`: the 4 experts of a token differ. Among the routes of the 128 tokens of one device no expert is named more than 10 times, and in every draw some expert is named exactly 10 times by the tokens of some device.
All inputs are finite; a program needn't handle non-finite values.
Results may differ from the reference program's by a relative error of at most 0.014.
Values may be sent and summed in bfloat16 or wider, within the bound.
No kernel may reach another device: no remote copies, remote signals or barrier semaphores. Data moves between devices by JAX's collectives and lax.ppermute only.
A program may use at most 64 MiB of HBM per device.

```python
import math
import jax
import jax.numpy as jnp
import numpy as np
from jax import lax

D = 1024
FF = 768
HEADS = 8
HEAD_DIM = 128
TOP = 4
GROUP = 32
TOK_DEV = 128
EXPERTS = 64
CAP = 10
MOST_THINK = 8
TOKENS = 65536
THINKERS = 4096
NCHUNK = 2048
N_SEQ = 8
N_EXP = 64


def draw_queries(key, part):
    key = jax.random.fold_in(key, 3)
    return (1.4 * jax.random.normal(key, (TOKENS, HEADS * HEAD_DIM), jnp.float32)).astype(jnp.bfloat16)


def draw_thinker_keys(key, part):
    key = jax.random.fold_in(key, 5)
    return (1.4 * jax.random.normal(key, (THINKERS, HEAD_DIM), jnp.float32)).astype(jnp.bfloat16)


def steps_of(stream_key, extent, cuts, low, top_value):
    def one(position, blocks):
        heights = jax.random.uniform(jax.random.fold_in(jax.random.fold_in(stream_key, 6), position), (blocks,), jnp.float32, low / len(cuts), top_value / len(cuts))
        return jnp.repeat(jnp.exp(heights), extent[position] // blocks).reshape((-1,) + (1,) * (len(extent) - position - 1))

    gain = one(*cuts[0])
    for cut in cuts[1:]:
        gain = gain * one(*cut)
    return gain


def length_profile(amount, total, reach, skew):
    portions = [(1 << 20) // math.isqrt(standing ** skew) + 1 for standing in range(2, amount + 1)]
    spare, holding = total - reach - (amount - 1), [1] * (amount - 1)
    while spare > 0:
        candidates = [i for i in range(amount - 1) if holding[i] < reach]
        mass, remaining = sum([portions[i] for i in candidates]), spare
        for i in candidates:
            more = min(reach - holding[i], max(1, remaining * portions[i] // mass), spare)
            holding[i] = holding[i] + more
            spare = spare - more
    return np.array([reach] + holding)


def uneven(rng, count, total, bound, slope):
    if count == 2:
        one = jax.random.randint(rng, (), max(1, total - bound), min(bound, total - 1) + 1)
        return jnp.stack([one, total - one])
    tallies = jnp.asarray(length_profile(count, total, bound, slope), jnp.int32)
    couples = (count - 1) // 2
    donor, sink = tallies[1:1 + 2 * couples:2], tallies[2:2 + 2 * couples:2]
    slack = jnp.minimum(donor - 1, bound - sink)
    moved = jax.random.randint(jax.random.fold_in(rng, 1), (couples,), 0, 1 << 20) % (slack + 1)
    tallies = tallies.at[1:1 + 2 * couples:2].set(donor - moved).at[2:2 + 2 * couples:2].set(sink + moved)
    return tallies[jax.random.permutation(jax.random.fold_in(rng, 2), count)]


def shared_out(own_key, own, number, rows, number_of, top, reach, slope):
    sequence = jax.random.permutation(own_key, number_of)
    packed, common = portions_of(number_of, rows * top, reach, slope, True), portions_of(number_of, rows * top, reach, slope, False)
    places = jnp.arange(number_of)

    def named(tallies, rotation):
        used = int((tallies > 0).sum())
        fixed = max(1, used // 4)
        passed = fixed + (places - fixed + rotation * (used - fixed)) % max(1, number_of - fixed)
        return jnp.zeros((number_of,), jnp.int32).at[sequence[jnp.where(places < fixed, places, passed)]].set(jnp.asarray(tallies, jnp.int32))

    tallies = jnp.where(number % 4 == 0, named(packed, number // 4), named(common, number - number // 4 - 1))
    mixed = jax.random.permutation(jax.random.fold_in(own, 3), number_of)
    giver, receiver = mixed[0:number_of // 2 * 2:2], mixed[1:number_of // 2 * 2:2]
    room = jnp.minimum(tallies[giver] - 1, reach - tallies[receiver]) // 2
    room = jnp.where((giver == sequence[0]) | (receiver == sequence[0]) | (tallies[receiver] == 0), 0, jnp.maximum(room, 0))
    passed = jax.random.randint(jax.random.fold_in(own, 4), (number_of // 2,), 0, 1 << 20) % (room + 1)
    tallies = tallies.at[giver].add(-passed).at[receiver].add(passed)
    items = jnp.searchsorted(jnp.cumsum(tallies), jnp.arange(rows * top), side="right").astype(jnp.int32)
    grid = items.reshape(top, rows).T
    grid = grid[jax.random.permutation(jax.random.fold_in(own, 1), rows)]
    rotation = jax.random.randint(jax.random.fold_in(own, 2), (rows, 1), 0, top)
    return jnp.take_along_axis(grid, (jnp.arange(top)[None, :] + rotation) % top, axis=1)


def portions_of(amount, total, limit, lean, full):
    weights = [(1 << 20) // math.isqrt(rank ** lean) + 1 for rank in range(1, amount + 1)]
    largest = limit if full else min(limit, max(-(-total // amount), total * weights[0] // sum(weights)))
    least = 1 if total - largest >= amount - 1 else 0
    counts, spare = [largest] + [least] * (amount - 1), total - largest - least * (amount - 1)
    while spare > 0:
        free = [i for i in range(1, amount) if counts[i] < largest] or [i for i in range(1, amount) if counts[i] < limit]
        whole, left = sum([weights[i] for i in free]), spare
        for i in free:
            extra = min(limit - counts[i], max(1, left * weights[i] // whole), spare)
            counts[i] = counts[i] + extra
            spare = spare - extra
    return np.array(counts)


def bell_draw(rng, extent, deviation, reach, cuts=(), kind=jnp.bfloat16):
    drawn = jax.random.normal(rng, extent, jnp.float32) * deviation
    if len(cuts) > 0:
        drawn = steps_of(rng, extent, cuts, -0.22, 0.18) * drawn
    return jnp.clip(drawn, min=-reach, max=reach).astype(kind)


def setup_inputs(seed: int = 0) -> dict:
    streams_of = jax.random.split(jax.random.key(seed), 13)
    hidden = bell_draw(streams_of[0], (TOKENS, D), 1.0, 6.0, ((0, 512),))
    queries = draw_queries(jax.random.fold_in(streams_of[12], 71), 0)
    thinker_keys = draw_thinker_keys(jax.random.fold_in(streams_of[12], 71), 0)
    thinker_values = bell_draw(streams_of[3], (THINKERS, HEAD_DIM), 3.0, 15.0, ((0, 512),))
    thinker_lengths = uneven(streams_of[4], NCHUNK, THINKERS, MOST_THINK, 2).astype(jnp.int32)
    out_proj = bell_draw(streams_of[5], (HEADS * HEAD_DIM, D), (HEADS * HEAD_DIM) ** -0.5, 0.1875)
    expert_ids_keys = jax.random.split(jax.random.fold_in(streams_of[6], 1), TOKENS // TOK_DEV)
    expert_ids_turns = jax.random.permutation(jax.random.fold_in(streams_of[6], 3), TOKENS // TOK_DEV)
    expert_ids = jax.vmap(lambda own, number: shared_out(jax.random.fold_in(streams_of[6], 2), own, number, TOK_DEV, EXPERTS, TOP, CAP, 1))(expert_ids_keys, expert_ids_turns).reshape((TOKENS, TOP))
    gate_values = jnp.clip(0.099609375 + 0.9003906 * jax.random.uniform(streams_of[7], (TOKENS, TOP), jnp.float32) ** steps_of(streams_of[7], (TOKENS, TOP), ((0, 512),), -0.2, 0.2), 0.099609375, 1.0).astype(jnp.bfloat16)
    w_gate = bell_draw(streams_of[8], (EXPERTS, D, FF), D ** -0.5, 0.1875, ((0, 64), (1, 8)))
    w_up = bell_draw(streams_of[9], (EXPERTS, D, FF), D ** -0.5, 0.1875, ((0, 64), (1, 8)))
    w_down = bell_draw(streams_of[10], (EXPERTS, FF, D), FF ** -0.5, 0.21875, ((0, 64), (2, 8)))
    cotangent = bell_draw(streams_of[11], (TOKENS, D), 0.4, 2.5, ((0, 512),))
    return dict(hidden=hidden, queries=queries, thinker_keys=thinker_keys, thinker_values=thinker_values, thinker_lengths=thinker_lengths, out_proj=out_proj, expert_ids=expert_ids, gate_values=gate_values, w_gate=w_gate, w_up=w_up, w_down=w_down, cotangent=cotangent)


NEG_FILL = -1.0e30


def attend_block(query_block, limit_block, key_table, value_table, score_scale):
    scores = jnp.einsum("thd,jd->thj", query_block.astype(jnp.float32), key_table.astype(jnp.float32)) * score_scale
    positions = jnp.arange(key_table.shape[0], dtype=jnp.int32)
    is_valid = positions[None, None, :] < limit_block[:, None, None]
    scores = jnp.where(is_valid, scores, NEG_FILL)
    row_max = jnp.max(scores, axis=2, keepdims=True)
    exponent = jnp.where(is_valid, jnp.exp(scores - row_max), 0.0)
    totals = jnp.sum(exponent, axis=2)
    weights = lax.optimization_barrier(exponent.astype(jnp.bfloat16))
    summed = jnp.einsum("thj,jd->thd", weights.astype(jnp.float32), value_table.astype(jnp.float32))
    return (summed / totals[:, :, None]).astype(jnp.bfloat16)


def reference(hidden, queries, thinker_keys, thinker_values, thinker_lengths, out_proj, expert_ids, gate_values, w_gate, w_up, w_down, cotangent):
    score_scale = HEAD_DIM ** -0.5
    group_ends = jnp.cumsum(thinker_lengths).astype(jnp.int32)
    limits = jnp.repeat(group_ends, GROUP, total_repeat_length=TOKENS)
    query_blocks = queries.reshape(TOKENS // 512, 512, HEADS, HEAD_DIM)
    limit_blocks = limits.reshape(TOKENS // 512, 512)
    attended = lax.map(lambda pair: attend_block(pair[0], pair[1], thinker_keys, thinker_values, score_scale), (query_blocks, limit_blocks))
    attended = attended.reshape(TOKENS, HEADS * HEAD_DIM)
    mixed = (hidden.astype(jnp.float32) + jnp.dot(attended, out_proj, preferred_element_type=jnp.float32)).astype(jnp.bfloat16)

    device_count = N_SEQ * N_EXP
    per_block = TOK_DEV * TOP
    id_blocks = expert_ids.reshape(device_count, per_block)
    onehot = (id_blocks[:, :, None] == jnp.arange(EXPERTS, dtype=jnp.int32)[None, None, :]).astype(jnp.int32)
    slot_rank = jnp.sum((jnp.cumsum(onehot, axis=1) - onehot) * onehot, axis=2).astype(jnp.int32)
    slot_column = (jnp.arange(device_count, dtype=jnp.int32)[:, None] * CAP + slot_rank).reshape(-1)
    route_table = jnp.full((EXPERTS, device_count * CAP), -1, jnp.int32)
    route_table = route_table.at[expert_ids.reshape(-1), slot_column].set(jnp.arange(TOKENS * TOP, dtype=jnp.int32))
    gate_flat = gate_values.reshape(-1)

    def per_expert(running, inputs):
        grad_acc, gates_acc = running
        table_row, gate_weight, up_weight, down_weight = inputs
        filled = table_row >= 0
        route_safe = jnp.where(filled, table_row, 0).astype(jnp.int32)
        token_safe = (route_safe // TOP).astype(jnp.int32)
        slot_rows = jnp.where(filled[:, None], mixed[token_safe], jnp.zeros((), jnp.bfloat16))
        cot_rows = jnp.where(filled[:, None], cotangent[token_safe], jnp.zeros((), jnp.bfloat16))
        gates_in = jnp.where(filled, gate_flat[route_safe], jnp.zeros((), jnp.bfloat16)).astype(jnp.float32)
        gate_lin = jnp.dot(slot_rows, gate_weight, preferred_element_type=jnp.float32)
        up_lin = jnp.dot(slot_rows, up_weight, preferred_element_type=jnp.float32)
        down_back = jnp.dot(cot_rows, down_weight.T, preferred_element_type=jnp.float32)
        sigmoid_gate = jax.nn.sigmoid(gate_lin)
        swish_gate = gate_lin * sigmoid_gate
        activation = swish_gate * up_lin
        gate_grad = jnp.sum(activation * down_back, axis=1).astype(jnp.bfloat16)
        act_grad = gates_in[:, None] * down_back
        gate_back = (act_grad * up_lin * sigmoid_gate * (1.0 + gate_lin * (1.0 - sigmoid_gate))).astype(jnp.bfloat16)
        up_back = (act_grad * swish_gate).astype(jnp.bfloat16)
        route_grad = (jnp.dot(gate_back, gate_weight.T, preferred_element_type=jnp.float32) + jnp.dot(up_back, up_weight.T, preferred_element_type=jnp.float32)).astype(jnp.bfloat16)
        grad_acc = grad_acc.at[token_safe].add(jnp.where(filled[:, None], route_grad.astype(jnp.float32), 0.0))
        gates_acc = gates_acc.at[route_safe].add(jnp.where(filled, gate_grad.astype(jnp.float32), 0.0))
        return (grad_acc, gates_acc), None

    start_acc = (jnp.zeros((TOKENS, D), jnp.float32), jnp.zeros((TOKENS * TOP,), jnp.float32))
    (grad_input, gates_acc), unused = lax.scan(per_expert, start_acc, (route_table, w_gate, w_up, w_down))
    grad_gates = gates_acc.reshape(TOKENS, TOP).astype(jnp.bfloat16)
    return grad_input, grad_gates
```

```python
import functools

import jax
import jax.numpy as jnp
from jax import lax
from jax.experimental import pallas as pl
from jax.experimental.pallas import tpu as pltpu
from jax.sharding import PartitionSpec as P

GROUP = 32
NEG = -1e30
LANES = 128
F32 = jnp.float32
BF16 = jnp.bfloat16
MIB = 1 << 20


def params(mib):
    return pltpu.CompilerParams(vmem_limit_bytes=mib * MIB)


def vmem(count):
    return [pl.BlockSpec(memory_space=pltpu.VMEM)] * count


SMEM = pl.BlockSpec(memory_space=pltpu.SMEM)


def iota(shape, dim):
    return lax.broadcasted_iota(jnp.int32, shape, dim)


def dot(a, b, dims=((1,), (0,))):
    return lax.dot_general(a, b, (dims, ((), ())), preferred_element_type=F32)


def as_bf16(mask):
    return jnp.where(mask, 1.0, 0.0).astype(BF16)


def fold_matrix(slots, chunks):
    rows = slots * chunks
    row, col = iota((rows, rows), 0), iota((rows, rows), 1)
    return as_bf16((row // chunks) + (row % chunks) * slots == col)


def unfold_matrix(slots, chunks):
    rows = slots * chunks
    row, col = iota((rows, rows), 0), iota((rows, rows), 1)
    return as_bf16((col // chunks) + (col % chunks) * slots == row)


BLOCK = 32


def fold_rows(wide, matrix, store):
    chunks = wide.shape[1] // LANES
    size = BLOCK * chunks

    def stacked(b):
        part = wide[b * BLOCK : (b + 1) * BLOCK, :]
        return jnp.concatenate(
            [part[:, c * LANES : (c + 1) * LANES] for c in range(chunks)], axis=0
        )

    for b in range(0, wide.shape[0] // BLOCK, 2):
        two = jnp.concatenate([stacked(b), stacked(b + 1)], axis=1)
        out = dot(matrix, two).astype(BF16)
        store(b * size, out[:, :LANES])
        store((b + 1) * size, out[:, LANES:])


def unfold_rows(load, slots, chunks, matrix, ref):
    size = BLOCK * chunks
    for b in range(0, slots // BLOCK, 2):
        two = jnp.concatenate([load(b * size, size), load((b + 1) * size, size)], axis=1)
        out = dot(matrix, two).astype(BF16)
        for half in range(2):
            for c in range(chunks):
                ref[
                    (b + half) * BLOCK : (b + half + 1) * BLOCK, c * LANES : (c + 1) * LANES
                ] = out[c * BLOCK : (c + 1) * BLOCK, half * LANES : (half + 1) * LANES]


def pack_kernel(lens_ref, key_ref, value_ref, out_ref):
    copies = out_ref.shape[0]
    total = lens_ref[0]
    for i in range(1, lens_ref.shape[0]):
        total = total + lens_ref[i]
    rows = key_ref.shape[0]
    tot = jnp.full((rows, LANES), total.astype(F32), F32).astype(BF16)
    one = jnp.concatenate([key_ref[...], value_ref[...], tot], axis=1)
    out_ref[...] = jnp.broadcast_to(one[None], (copies,) + one.shape)


def segment_kernel(in_ref, out_ref, *, rows):
    count = in_ref.shape[0]
    out_ref[0:count, :] = in_ref[:, 0 : 2 * LANES]
    tot = in_ref[:, 2 * LANES :].astype(F32)
    row, lane = iota(tot.shape, 0), iota(tot.shape, 1)
    line = jnp.sum(jnp.where(row == lane * rows, tot, 0.0), axis=0, keepdims=True)
    more = out_ref.shape[0] - count
    line = jnp.broadcast_to(line, (more, LANES))
    out_ref[count:, :] = jnp.concatenate([line, jnp.zeros_like(line)], axis=1).astype(BF16)


def placed(slot_rows, top, slots, values=None):
    tokens = slot_rows.shape[1]
    place = iota((slots, tokens), 0)
    out = jnp.zeros((slots, tokens), F32)
    for k in range(top):
        value = 1.0 if values is None else values[k : k + 1, :]
        out = jnp.where(place == slot_rows[k : k + 1, :], value, out)
    return out.astype(BF16)


def dispatch_kernel(ids_ref, gate_ref, cot_ref, slot_ref, send_ref, *, experts, capacity):
    top, tokens = ids_ref.shape
    ids = ids_ref[...]
    expert = iota((experts, tokens), 0)
    named = jnp.zeros((experts, tokens), F32)
    for k in range(top):
        named = jnp.where(expert == ids[k : k + 1, :], 1.0, named)
    earlier = as_bf16(iota((tokens, tokens), 0) < iota((tokens, tokens), 1))
    before = dot(named.astype(BF16), earlier)
    slot_rows, ranks = [], []
    for k in range(top):
        own = ids[k : k + 1, :]
        rank = jnp.sum(jnp.where(expert == own, before, 0.0), axis=0, keepdims=True)
        rank = rank.astype(jnp.int32)
        ranks.append(rank)
        slot_rows.append(own * capacity + rank)
    both = jnp.concatenate(slot_rows + ranks, axis=0)
    slot_ref[...] = both
    slots = experts * capacity
    spread = placed(both, top, slots, gate_ref[...].astype(F32))
    wide = dot(spread, cot_ref[...]).astype(BF16)
    chunks = cot_ref.shape[1] // LANES

    def store(first, rows):
        send_ref[first : first + rows.shape[0], :] = rows

    fold_rows(wide, fold_matrix(BLOCK, chunks), store)


def attend_kernel(
    place_ref,
    lens_ref,
    kv_ref,
    query_ref,
    hidden_ref,
    proj_ref,
    slot_ref,
    send_ref,
    max_ref,
    acc_ref,
    *,
    segments,
    rows,
    pitch,
    top,
):
    tokens = query_ref.shape[0]
    heads = query_ref.shape[1] // LANES
    seq, exp = place_ref[0], place_ref[1]
    total = jnp.zeros((16, LANES), F32)
    lane = iota((16, LANES), 1)
    for s in range(segments):
        line = kv_ref[s * pitch + rows : s * pitch + rows + 16, 0:LANES].astype(F32)
        take = jnp.logical_or(seq > s, jnp.logical_and(seq == s, lane < exp))
        total = total + jnp.where(take, line, 0.0)
    offset = (jnp.sum(total) * (1.0 / 16.0)).astype(jnp.int32)
    ends = []
    for g in range(lens_ref.shape[0]):
        offset = offset + lens_ref[g]
        ends.append(offset)
    group = iota((tokens, 1), 0) // GROUP
    limits = jnp.zeros((tokens, 1), jnp.int32)
    for g, end in enumerate(ends):
        limits = jnp.where(group == g, end, limits)
    scale = LANES**-0.5 * 1.4426950408889634
    max_ref[...] = jnp.full(max_ref.shape, NEG, F32)
    acc_ref[...] = jnp.zeros(acc_ref.shape, F32)
    ones = as_bf16(iota((rows, LANES), 1) == 0)

    def block(masked):
        def body(b, carry):
            first = pl.multiple_of(b * pitch, 16)
            keys = kv_ref[pl.ds(first, rows), 0:LANES]
            values = kv_ref[pl.ds(first, rows), LANES : 2 * LANES]
            wide = jnp.concatenate([values, ones], axis=1)
            for h in range(heads):
                q = query_ref[:, h * LANES : (h + 1) * LANES]
                s = dot(q, keys, ((1,), (1,)))
                if masked:
                    seen = iota((tokens, rows), 1) + b * rows < limits
                    s = jnp.where(seen, s, NEG)
                old = max_ref[h]
                new = jnp.maximum(old, jnp.max(s, axis=1, keepdims=True))
                max_ref[h] = new
                w = jnp.exp2((s - new) * scale).astype(BF16)
                factor = jnp.exp2((old - new) * scale)
                acc_ref[h] = acc_ref[h] * factor + dot(w, wide)
            return carry

        return body

    full = ends[0] // rows
    last = (ends[-1] + rows - 1) // rows
    lax.fori_loop(0, full, block(False), 0)
    lax.fori_loop(full, last, block(True), 0)
    attended = []
    for h in range(heads):
        acc = acc_ref[h]
        attended.append((acc[:, :LANES] / acc[:, LANES : LANES + 1]).astype(BF16))
    mixed = hidden_ref[...].astype(F32) + dot(jnp.concatenate(attended, axis=1), proj_ref[...])
    chunks = hidden_ref.shape[1] // LANES
    slots = send_ref.shape[0] // chunks
    wide = dot(placed(slot_ref[...], top, slots), mixed.astype(BF16)).astype(BF16)

    def store(first, part):
        send_ref[first : first + part.shape[0], :] = part

    fold_rows(wide, fold_matrix(BLOCK, chunks), store)


def expert_kernel(
    row_ref, cot_ref, weight_ref, out_ref, x_ref, c_ref, grad_ref, *, shards, ff, capacity
):
    slots, width = x_ref.shape
    chunks = width // LANES
    matrix = unfold_matrix(BLOCK, chunks)
    unfold_rows(lambda f, n: row_ref[f : f + n, :], slots, chunks, matrix, x_ref)
    unfold_rows(lambda f, n: cot_ref[f : f + n, :], slots, chunks, matrix, c_ref)
    x, c = x_ref[...], c_ref[...]
    pitch = weight_ref.shape[0] // shards
    step = 256
    gate_sum = jnp.zeros((slots, 1), F32)

    def columns(base, j):
        return jnp.concatenate(
            [
                jnp.concatenate(
                    [
                        weight_ref[
                            s * pitch + base + (j * 2 + i) * LANES : s * pitch
                            + base
                            + (j * 2 + i + 1) * LANES,
                            :,
                        ]
                        for i in range(2)
                    ],
                    axis=1,
                )
                for s in range(shards)
            ],
            axis=0,
        )

    for j in range(ff // step):
        w_gate, w_up = columns(0, j), columns(ff, j)
        w_down = jnp.concatenate(
            [
                weight_ref[s * pitch + 2 * ff + j * step : s * pitch + 2 * ff + (j + 1) * step, :]
                for s in range(shards)
            ],
            axis=1,
        )
        gate_lin = dot(x, w_gate)
        up_lin = dot(x, w_up)
        back = dot(c, w_down, ((1,), (1,)))
        sig = 1.0 / (1.0 + jnp.exp(-gate_lin))
        swish = gate_lin * sig
        up_back = back * swish
        gate_sum = gate_sum + jnp.sum(up_back * up_lin, axis=1, keepdims=True)
        gate_back = back * up_lin * sig * (1.0 + gate_lin * (1.0 - sig))
        part = dot(gate_back.astype(BF16), w_gate, ((1,), (1,))) + dot(
            up_back.astype(BF16), w_up, ((1,), (1,))
        )
        if j == 0:
            grad_ref[...] = part
        else:
            grad_ref[...] += part
    experts = slots // capacity
    each = capacity * chunks

    def store(first, rows):
        size = rows.shape[0]
        at = first
        while at < first + size:
            e, r = at // each, at % each
            n = min(each - r, first + size - at)
            out_ref[e, r : r + n, :] = rows[at - first : at - first + n, :]
            at += n

    fold_rows(grad_ref[...].astype(BF16), fold_matrix(BLOCK, chunks), store)
    high = gate_sum.astype(BF16)
    low = (gate_sum - high.astype(F32)).astype(BF16)
    slot, lane = iota((slots, LANES), 0), iota((slots, LANES), 1)
    rank = slot % capacity
    spread = jnp.where(rank == lane, high.astype(F32), 0.0) + jnp.where(
        rank + 16 == lane, low.astype(F32), 0.0
    )
    owner = as_bf16(iota((experts, slots), 0) == iota((experts, slots), 1) // capacity)
    lines = dot(owner, spread.astype(BF16)).astype(BF16)
    for e in range(experts):
        out_ref[e, each:, :] = jnp.broadcast_to(
            lines[e : e + 1, :], (out_ref.shape[1] - each, LANES)
        )


def combine_kernel(
    back_ref, line_ref, ids_ref, gate_ref, slot_ref, grad_ref, gates_ref, wide_ref, *, capacity
):
    top, tokens = ids_ref.shape
    slots, width = wide_ref.shape
    chunks = width // LANES
    experts = slots // capacity
    each = capacity * chunks

    def load(first, count):
        parts, at = [], first
        while at < first + count:
            e, r = at // each, at % each
            n = min(each - r, first + count - at)
            parts.append(back_ref[e, r : r + n, :])
            at += n
        return jnp.concatenate(parts, axis=0)

    unfold_rows(load, slots, chunks, unfold_matrix(BLOCK, chunks), wide_ref)
    both = slot_ref[...]
    spread = placed(both, top, slots)
    grad_ref[...] = dot(spread, wide_ref[...], ((0,), (0,)))
    lines = line_ref[...]
    expert = iota((experts, tokens), 0)
    rank = iota((LANES, tokens), 0)
    out = []
    for k in range(top):
        own = as_bf16(expert == ids_ref[k : k + 1, :])
        found = dot(lines, own, ((0,), (0,)))
        mine = both[top + k : top + k + 1, :]
        take = jnp.logical_or(rank == mine, rank == mine + 16)
        value = jnp.sum(jnp.where(take, found, 0.0), axis=0, keepdims=True)
        out.append(value / gate_ref[k : k + 1, :].astype(F32))
    gates_ref[...] = jnp.concatenate(out, axis=0).astype(BF16)


def exchange(rows):
    return lax.all_to_all(rows, "exp", split_axis=0, concat_axis=0, tiled=True)


def local(
    hidden,
    queries,
    thinker_keys,
    thinker_values,
    thinker_lengths,
    out_proj,
    expert_ids,
    gate_values,
    w_gate,
    w_up,
    w_down,
    cotangent,
):
    tokens, width = hidden.shape
    top = expert_ids.shape[1]
    experts, shards = lax.axis_size("exp"), lax.axis_size("seq")
    capacity = tokens * top * 5 // (4 * experts)
    slots = experts * capacity
    chunks = width // LANES
    each = capacity * chunks
    ff = w_gate.shape[2]
    own_rows = thinker_keys.shape[0]
    rows = experts * own_rows
    pitch = rows + 16
    place = jnp.stack([lax.axis_index("seq"), lax.axis_index("exp")]).astype(jnp.int32)
    ids, gates = expert_ids.T, gate_values.T

    packed = pl.pallas_call(
        pack_kernel,
        out_shape=jax.ShapeDtypeStruct((experts, own_rows, 3 * LANES), BF16),
        in_specs=[SMEM] + vmem(2),
        out_specs=vmem(1)[0],
        compiler_params=params(16),
        name="pack",
    )(thinker_lengths, thinker_keys, thinker_values)
    kv_rows = exchange(packed)

    slot_table, send_cot = pl.pallas_call(
        functools.partial(dispatch_kernel, experts=experts, capacity=capacity),
        out_shape=(
            jax.ShapeDtypeStruct((2 * top, tokens), jnp.int32),
            jax.ShapeDtypeStruct((slots * chunks, LANES), BF16),
        ),
        in_specs=vmem(3),
        out_specs=tuple(vmem(2)),
        compiler_params=params(24),
        name="dispatch",
    )(ids, gates, cotangent)

    segment = pl.pallas_call(
        functools.partial(segment_kernel, rows=own_rows),
        out_shape=jax.ShapeDtypeStruct((pitch, 2 * LANES), BF16),
        in_specs=vmem(1),
        out_specs=vmem(1)[0],
        compiler_params=params(16),
        name="segment",
    )(kv_rows.reshape(rows, 3 * LANES))
    segment, send_cot = lax.optimization_barrier((segment, send_cot))
    kv_all = lax.all_gather(segment, "seq", axis=0, tiled=True)
    recv_cot = exchange(send_cot.reshape(experts, each, LANES))

    def blocks(w):
        return w[0].reshape(LANES, ff // LANES, LANES).transpose(1, 0, 2).reshape(ff, LANES)

    shard = jnp.concatenate([blocks(w_gate), blocks(w_up), w_down[0]], axis=0)
    kv_all, shard = lax.optimization_barrier((kv_all, shard))
    weights = lax.all_gather(shard, "seq", axis=0, tiled=True)

    send_rows = pl.pallas_call(
        functools.partial(attend_kernel, segments=shards, rows=rows, pitch=pitch, top=top),
        out_shape=jax.ShapeDtypeStruct((slots * chunks, LANES), BF16),
        in_specs=[SMEM, SMEM] + vmem(5),
        out_specs=vmem(1)[0],
        scratch_shapes=[
            pltpu.VMEM((width // LANES, tokens, 1), F32),
            pltpu.VMEM((width // LANES, tokens, 2 * LANES), F32),
        ],
        compiler_params=params(32),
        name="attend",
    )(place, thinker_lengths, kv_all, queries, hidden, out_proj, slot_table)
    send_rows, recv_cot = lax.optimization_barrier((send_rows, recv_cot))
    recv_rows = exchange(send_rows.reshape(experts, each, LANES))

    back = pl.pallas_call(
        functools.partial(expert_kernel, shards=shards, ff=ff, capacity=capacity),
        out_shape=jax.ShapeDtypeStruct((experts, each + 8, LANES), BF16),
        in_specs=vmem(3),
        out_specs=vmem(1)[0],
        scratch_shapes=[
            pltpu.VMEM((slots, width), BF16),
            pltpu.VMEM((slots, width), BF16),
            pltpu.VMEM((slots, width), F32),
        ],
        compiler_params=params(48),
        name="expert",
    )(recv_rows.reshape(slots * chunks, LANES), recv_cot.reshape(slots * chunks, LANES), weights)
    home = exchange(back)

    grad_input, grad_gates = pl.pallas_call(
        functools.partial(combine_kernel, capacity=capacity),
        out_shape=(
            jax.ShapeDtypeStruct((tokens, width), F32),
            jax.ShapeDtypeStruct((top, tokens), BF16),
        ),
        in_specs=vmem(5),
        out_specs=tuple(vmem(2)),
        scratch_shapes=[pltpu.VMEM((slots, width), BF16)],
        compiler_params=params(24),
        name="combine",
    )(home, home[:, each, :], ids, gates, slot_table)
    return grad_input, grad_gates.T


def solution(mesh):
    both = P(("seq", "exp"), None)
    return jax.shard_map(
        local,
        mesh=mesh,
        in_specs=(
            both,
            both,
            both,
            both,
            P(("seq", "exp")),
            P(),
            both,
            both,
            P("exp", "seq", None),
            P("exp", "seq", None),
            P("exp", None, "seq"),
            both,
        ),
        out_specs=(both, both),
        check_vma=False,
    )
```

```python
import functools

import jax
import jax.numpy as jnp
from jax import lax
from jax.experimental import pallas as pl
from jax.experimental.pallas import tpu as pltpu
from jax.sharding import PartitionSpec as P

GROUP = 32
NEG = -1e30
LANES = 128
F32 = jnp.float32
BF16 = jnp.bfloat16
MIB = 1 << 20


def params(mib):
    return pltpu.CompilerParams(vmem_limit_bytes=mib * MIB)


def vmem(count):
    return [pl.BlockSpec(memory_space=pltpu.VMEM)] * count


SMEM = pl.BlockSpec(memory_space=pltpu.SMEM)


def iota(shape, dim):
    return lax.broadcasted_iota(jnp.int32, shape, dim)


def dot(a, b, dims=((1,), (0,))):
    return lax.dot_general(a, b, (dims, ((), ())), preferred_element_type=F32)


def as_bf16(mask):
    return jnp.where(mask, 1.0, 0.0).astype(BF16)


def fold_matrix(slots, chunks):
    rows = slots * chunks
    row, col = iota((rows, rows), 0), iota((rows, rows), 1)
    return as_bf16((row // chunks) + (row % chunks) * slots == col)


def unfold_matrix(slots, chunks):
    rows = slots * chunks
    row, col = iota((rows, rows), 0), iota((rows, rows), 1)
    return as_bf16((col // chunks) + (col % chunks) * slots == row)


BLOCK = 32


def fold_rows(wide, matrix, store):
    chunks = wide.shape[1] // LANES
    size = BLOCK * chunks

    def stacked(b):
        part = wide[b * BLOCK : (b + 1) * BLOCK, :]
        return jnp.concatenate(
            [part[:, c * LANES : (c + 1) * LANES] for c in range(chunks)], axis=0
        )

    for b in range(0, wide.shape[0] // BLOCK, 2):
        two = jnp.concatenate([stacked(b), stacked(b + 1)], axis=1)
        out = dot(matrix, two).astype(BF16)
        store(b * size, out[:, :LANES])
        store((b + 1) * size, out[:, LANES:])


def unfold_rows(load, slots, chunks, matrix, ref):
    size = BLOCK * chunks
    for b in range(0, slots // BLOCK, 2):
        two = jnp.concatenate([load(b * size, size), load((b + 1) * size, size)], axis=1)
        out = dot(matrix, two).astype(BF16)
        for half in range(2):
            for c in range(chunks):
                ref[
                    (b + half) * BLOCK : (b + half + 1) * BLOCK, c * LANES : (c + 1) * LANES
                ] = out[c * BLOCK : (c + 1) * BLOCK, half * LANES : (half + 1) * LANES]


def pack_kernel(lens_ref, key_ref, value_ref, out_ref):
    copies = out_ref.shape[0]
    total = lens_ref[0]
    for i in range(1, lens_ref.shape[0]):
        total = total + lens_ref[i]
    rows = key_ref.shape[0]
    tot = jnp.full((rows, LANES), total.astype(F32), F32).astype(BF16)
    one = jnp.concatenate([key_ref[...], value_ref[...], tot], axis=1)
    out_ref[...] = jnp.broadcast_to(one[None], (copies,) + one.shape)


def segment_kernel(in_ref, out_ref, *, rows):
    count = in_ref.shape[0]
    out_ref[0:count, :] = in_ref[:, 0 : 2 * LANES]
    tot = in_ref[:, 2 * LANES :].astype(F32)
    row, lane = iota(tot.shape, 0), iota(tot.shape, 1)
    line = jnp.sum(jnp.where(row == lane * rows, tot, 0.0), axis=0, keepdims=True)
    more = out_ref.shape[0] - count
    line = jnp.broadcast_to(line, (more, LANES))
    out_ref[count:, :] = jnp.concatenate([line, jnp.zeros_like(line)], axis=1).astype(BF16)


def placed(slot_rows, top, slots, values=None):
    tokens = slot_rows.shape[1]
    place = iota((slots, tokens), 0)
    out = jnp.zeros((slots, tokens), F32)
    for k in range(top):
        value = 1.0 if values is None else values[k : k + 1, :]
        out = jnp.where(place == slot_rows[k : k + 1, :], value, out)
    return out.astype(BF16)


def dispatch_kernel(ids_ref, gate_ref, cot_ref, slot_ref, send_ref, *, experts, capacity):
    top, tokens = ids_ref.shape
    ids = ids_ref[...]
    expert = iota((experts, tokens), 0)
    named = jnp.zeros((experts, tokens), F32)
    for k in range(top):
        named = jnp.where(expert == ids[k : k + 1, :], 1.0, named)
    earlier = as_bf16(iota((tokens, tokens), 0) < iota((tokens, tokens), 1))
    before = dot(named.astype(BF16), earlier)
    slot_rows, ranks = [], []
    for k in range(top):
        own = ids[k : k + 1, :]
        rank = jnp.sum(jnp.where(expert == own, before, 0.0), axis=0, keepdims=True)
        rank = rank.astype(jnp.int32)
        ranks.append(rank)
        slot_rows.append(own * capacity + rank)
    both = jnp.concatenate(slot_rows + ranks, axis=0)
    slot_ref[...] = both
    slots = experts * capacity
    spread = placed(both, top, slots, gate_ref[...].astype(F32))
    wide = dot(spread, cot_ref[...]).astype(BF16)
    chunks = cot_ref.shape[1] // LANES

    def store(first, rows):
        send_ref[first : first + rows.shape[0], :] = rows

    fold_rows(wide, fold_matrix(BLOCK, chunks), store)


def attend_kernel(
    place_ref,
    lens_ref,
    kv_ref,
    query_ref,
    hidden_ref,
    proj_ref,
    slot_ref,
    send_ref,
    max_ref,
    acc_ref,
    kv_buf,
    proj_buf,
    kv_sem,
    proj_sem,
    *,
    segments,
    rows,
    pitch,
    top,
    together,
):
    def kv_copy(b):
        return pltpu.make_async_copy(kv_ref.at[b], kv_buf.at[b], kv_sem.at[b])

    proj_copy = pltpu.make_async_copy(proj_ref, proj_buf, proj_sem)
    for b in range(segments):
        kv_copy(b).start()
    proj_copy.start()
    tokens = query_ref.shape[0]
    heads = query_ref.shape[1] // LANES
    scale = LANES**-0.5 * 1.4426950408889634
    max_ref[...] = jnp.full(max_ref.shape, NEG, F32)
    acc_ref[...] = jnp.zeros(acc_ref.shape, F32)
    for b in range(segments):
        kv_copy(b).wait()
    seq, exp = place_ref[0], place_ref[1]
    total = jnp.zeros((16, LANES), F32)
    lane = iota((16, LANES), 1)
    for s in range(segments):
        line = kv_buf[s, rows : rows + 16, 0:LANES].astype(F32)
        take = jnp.logical_or(seq > s, jnp.logical_and(seq == s, lane < exp))
        total = total + jnp.where(take, line, 0.0)
    offset = (jnp.sum(total) * (1.0 / 16.0)).astype(jnp.int32)
    ends = []
    for g in range(lens_ref.shape[0]):
        offset = offset + lens_ref[g]
        ends.append(offset)
    size = together * tokens
    group = (iota((size, 1), 0) % tokens) // GROUP
    limits = jnp.zeros((size, 1), jnp.int32)
    for g, end in enumerate(ends):
        limits = jnp.where(group == g, end, limits)
    ones = as_bf16(iota((rows, LANES), 1) == 0)

    def block(masked):
        def body(b, carry):
            keys = kv_buf[b, 0:rows, 0:LANES]
            wide = jnp.concatenate([kv_buf[b, 0:rows, LANES : 2 * LANES], ones], axis=1)
            for h in range(0, heads, together):
                q = jnp.concatenate(
                    [query_ref[:, i * LANES : (i + 1) * LANES] for i in range(h, h + together)],
                    axis=0,
                )
                at = slice(h * tokens, h * tokens + size)
                s = dot(q, keys, ((1,), (1,)))
                if masked:
                    s = jnp.where(iota((size, rows), 1) + b * rows < limits, s, NEG)
                old = max_ref[at, :]
                new = jnp.maximum(old, jnp.max(s, axis=1, keepdims=True))
                max_ref[at, :] = new
                w = jnp.exp2((s - new) * scale).astype(BF16)
                factor = jnp.exp2((old - new) * scale)
                acc_ref[at, :] = acc_ref[at, :] * factor + dot(w, wide)
            return carry

        return body

    full = ends[0] // rows
    last = (ends[-1] + rows - 1) // rows
    lax.fori_loop(0, full, block(False), 0)
    lax.fori_loop(full, last, block(True), 0)
    attended = []
    for h in range(heads):
        acc = acc_ref[h * tokens : (h + 1) * tokens, :]
        attended.append((acc[:, :LANES] / acc[:, LANES : LANES + 1]).astype(BF16))
    proj_copy.wait()
    mixed = hidden_ref[...].astype(F32) + dot(jnp.concatenate(attended, axis=1), proj_buf[...])
    chunks = hidden_ref.shape[1] // LANES
    slots = send_ref.shape[0] // chunks
    wide = dot(placed(slot_ref[...], top, slots), mixed.astype(BF16)).astype(BF16)

    def store(first, part):
        send_ref[first : first + part.shape[0], :] = part

    fold_rows(wide, fold_matrix(BLOCK, chunks), store)


def prepare_kernel(cot_ref, weight_ref, gate_ref, up_ref, back_ref, c_ref, *, shards, ff):
    slots, width = c_ref.shape
    chunks = width // LANES
    pitch = weight_ref.shape[0] // shards
    for s in range(shards):
        for i in range(ff // LANES):
            for base, ref in ((0, gate_ref), (ff, up_ref)):
                at = s * pitch + base + i * LANES
                ref[s * LANES : (s + 1) * LANES, i * LANES : (i + 1) * LANES] = weight_ref[
                    at : at + LANES, :
                ]
    unfold_rows(
        lambda f, n: cot_ref[f : f + n, :], slots, chunks, unfold_matrix(BLOCK, chunks), c_ref
    )
    c = c_ref[...]
    step = 256
    for j in range(ff // step):
        w_down = jnp.concatenate(
            [
                weight_ref[s * pitch + 2 * ff + j * step : s * pitch + 2 * ff + (j + 1) * step, :]
                for s in range(shards)
            ],
            axis=1,
        )
        back_ref[:, j * step : (j + 1) * step] = dot(c, w_down, ((1,), (1,)))


def expert_kernel(
    row_ref,
    gate_ref,
    up_ref,
    back_ref,
    out_ref,
    x_ref,
    grad_ref,
    gate_buf,
    up_buf,
    back_buf,
    other_sem,
    *,
    capacity,
):
    slots, width = x_ref.shape
    chunks = width // LANES
    ff = gate_ref.shape[1]
    others = [
        pltpu.make_async_copy(src, dst, other_sem.at[i])
        for i, (src, dst) in enumerate(
            ((gate_ref, gate_buf), (up_ref, up_buf), (back_ref, back_buf))
        )
    ]
    for copy in others:
        copy.start()
    unfold_rows(
        lambda f, n: row_ref[f : f + n, :], slots, chunks, unfold_matrix(BLOCK, chunks), x_ref
    )
    x = x_ref[...]
    for copy in others:
        copy.wait()
    step = 256
    gate_sum = jnp.zeros((slots, 1), F32)
    for j in range(ff // step):
        at = slice(j * step, (j + 1) * step)
        w_gate, w_up = gate_buf[:, at], up_buf[:, at]
        back = back_buf[:, at]
        gate_lin = dot(x, w_gate)
        up_lin = dot(x, w_up)
        sig = 0.5 * jnp.tanh(0.5 * gate_lin) + 0.5
        swish = gate_lin * sig
        up_back = back * swish
        gate_sum = gate_sum + jnp.sum(up_back * up_lin, axis=1, keepdims=True)
        gate_back = back * up_lin * (sig + swish * (1.0 - sig))
        part = dot(gate_back.astype(BF16), w_gate, ((1,), (1,))) + dot(
            up_back.astype(BF16), w_up, ((1,), (1,))
        )
        if j == 0:
            grad_ref[...] = part
        else:
            grad_ref[...] += part
    experts = slots // capacity
    each = capacity * chunks

    def store(first, rows):
        size = rows.shape[0]
        at = first
        while at < first + size:
            e, r = at // each, at % each
            n = min(each - r, first + size - at)
            out_ref[e, r : r + n, :] = rows[at - first : at - first + n, :]
            at += n

    fold_rows(grad_ref[...].astype(BF16), fold_matrix(BLOCK, chunks), store)
    high = gate_sum.astype(BF16)
    low = (gate_sum - high.astype(F32)).astype(BF16)
    slot, lane = iota((slots, LANES), 0), iota((slots, LANES), 1)
    rank = slot % capacity
    spread = jnp.where(rank == lane, high.astype(F32), 0.0) + jnp.where(
        rank + 16 == lane, low.astype(F32), 0.0
    )
    owner = as_bf16(iota((experts, slots), 0) == iota((experts, slots), 1) // capacity)
    lines = dot(owner, spread.astype(BF16)).astype(BF16)
    for e in range(experts):
        out_ref[e, each:, :] = jnp.broadcast_to(
            lines[e : e + 1, :], (out_ref.shape[1] - each, LANES)
        )


def combine_kernel(
    back_ref, line_ref, ids_ref, gate_ref, slot_ref, grad_ref, gates_ref, wide_ref, *, capacity
):
    top, tokens = ids_ref.shape
    slots, width = wide_ref.shape
    chunks = width // LANES
    experts = slots // capacity
    each = capacity * chunks

    def load(first, count):
        parts, at = [], first
        while at < first + count:
            e, r = at // each, at % each
            n = min(each - r, first + count - at)
            parts.append(back_ref[e, r : r + n, :])
            at += n
        return jnp.concatenate(parts, axis=0)

    unfold_rows(load, slots, chunks, unfold_matrix(BLOCK, chunks), wide_ref)
    both = slot_ref[...]
    spread = placed(both, top, slots)
    grad_ref[...] = dot(spread, wide_ref[...], ((0,), (0,)))
    lines = line_ref[...]
    expert = iota((experts, tokens), 0)
    rank = iota((LANES, tokens), 0)
    out = []
    for k in range(top):
        own = as_bf16(expert == ids_ref[k : k + 1, :])
        found = dot(lines, own, ((0,), (0,)))
        mine = both[top + k : top + k + 1, :]
        take = jnp.logical_or(rank == mine, rank == mine + 16)
        value = jnp.sum(jnp.where(take, found, 0.0), axis=0, keepdims=True)
        out.append(value / gate_ref[k : k + 1, :].astype(F32))
    gates_ref[...] = jnp.concatenate(out, axis=0).astype(BF16)


HBM = pl.BlockSpec(memory_space=pltpu.HBM)
TOGETHER = 2


def attend(place, lens, kv, queries, hidden, proj, slot_table, *, rows, slots):
    tokens, width = hidden.shape
    segments, pitch = kv.shape[0], kv.shape[1]
    top = slot_table.shape[0] // 2
    heads, chunks = queries.shape[1] // LANES, width // LANES
    return pl.pallas_call(
        functools.partial(
            attend_kernel, segments=segments, rows=rows, pitch=pitch, top=top, together=TOGETHER
        ),
        out_shape=jax.ShapeDtypeStruct((slots * chunks, LANES), BF16),
        in_specs=[SMEM, SMEM, HBM] + vmem(2) + [HBM] + vmem(1),
        out_specs=vmem(1)[0],
        scratch_shapes=[
            pltpu.VMEM((heads * tokens, 1), F32),
            pltpu.VMEM((heads * tokens, 2 * LANES), F32),
            pltpu.VMEM(kv.shape, BF16),
            pltpu.VMEM(proj.shape, BF16),
            pltpu.SemaphoreType.DMA((segments,)),
            pltpu.SemaphoreType.DMA(()),
        ],
        compiler_params=params(58),
        cost_estimate=pl.CostEstimate(flops=0, bytes_accessed=0, transcendentals=0),
        name="attend",
    )(place, lens, kv, queries, hidden, proj, slot_table)


def expert(rows, gate, up, back, *, capacity):
    slots, (width, ff) = back.shape[0], gate.shape
    chunks = width // LANES
    return pl.pallas_call(
        functools.partial(expert_kernel, capacity=capacity),
        out_shape=jax.ShapeDtypeStruct((slots // capacity, capacity * chunks + 8, LANES), BF16),
        in_specs=vmem(1) + [HBM] * 3,
        out_specs=vmem(1)[0],
        scratch_shapes=[
            pltpu.VMEM((slots, width), BF16),
            pltpu.VMEM((slots, width), F32),
            pltpu.VMEM(gate.shape, BF16),
            pltpu.VMEM(up.shape, BF16),
            pltpu.VMEM(back.shape, F32),
            pltpu.SemaphoreType.DMA((3,)),
        ],
        compiler_params=params(50),
        name="expert",
    )(rows, gate, up, back)


def exchange(rows):
    return lax.all_to_all(rows, "exp", split_axis=0, concat_axis=0, tiled=True)


def local(
    hidden,
    queries,
    thinker_keys,
    thinker_values,
    thinker_lengths,
    out_proj,
    expert_ids,
    gate_values,
    w_gate,
    w_up,
    w_down,
    cotangent,
):
    tokens, width = hidden.shape
    top = expert_ids.shape[1]
    experts, shards = lax.axis_size("exp"), lax.axis_size("seq")
    capacity = tokens * top * 5 // (4 * experts)
    slots = experts * capacity
    chunks = width // LANES
    each = capacity * chunks
    ff = w_gate.shape[2]
    own_rows = thinker_keys.shape[0]
    rows = experts * own_rows
    pitch = rows + 16
    place = jnp.stack([lax.axis_index("seq"), lax.axis_index("exp")]).astype(jnp.int32)
    ids, gates = expert_ids.T, gate_values.T

    packed = pl.pallas_call(
        pack_kernel,
        out_shape=jax.ShapeDtypeStruct((experts, own_rows, 3 * LANES), BF16),
        in_specs=[SMEM] + vmem(2),
        out_specs=vmem(1)[0],
        compiler_params=params(16),
        name="pack",
    )(thinker_lengths, thinker_keys, thinker_values)
    kv_rows = exchange(packed)

    slot_table, send_cot = pl.pallas_call(
        functools.partial(dispatch_kernel, experts=experts, capacity=capacity),
        out_shape=(
            jax.ShapeDtypeStruct((2 * top, tokens), jnp.int32),
            jax.ShapeDtypeStruct((slots * chunks, LANES), BF16),
        ),
        in_specs=vmem(3),
        out_specs=tuple(vmem(2)),
        compiler_params=params(24),
        name="dispatch",
    )(ids, gates, cotangent)

    segment = pl.pallas_call(
        functools.partial(segment_kernel, rows=own_rows),
        out_shape=jax.ShapeDtypeStruct((pitch, 2 * LANES), BF16),
        in_specs=vmem(1),
        out_specs=vmem(1)[0],
        compiler_params=params(16),
        name="segment",
    )(kv_rows.reshape(rows, 3 * LANES))
    def blocks(w):
        return w[0].reshape(LANES, ff // LANES, LANES).transpose(1, 0, 2).reshape(ff, LANES)

    shard = jnp.concatenate([blocks(w_gate), blocks(w_up), w_down[0]], axis=0)
    segment, send_cot, shard = lax.optimization_barrier((segment, send_cot, shard))
    kv_all = lax.all_gather(segment, "seq", axis=0, tiled=True)
    recv_cot = exchange(send_cot.reshape(experts, each, LANES))
    weights = lax.all_gather(shard, "seq", axis=0, tiled=True)

    send_rows = attend(
        place,
        thinker_lengths,
        kv_all.reshape(shards, pitch, 2 * LANES),
        queries,
        hidden,
        out_proj,
        slot_table,
        rows=rows,
        slots=slots,
    )
    send_rows, recv_cot = lax.optimization_barrier((send_rows, recv_cot))
    recv_rows = exchange(send_rows.reshape(experts, each, LANES))
    full_gate, full_up, down_back = pl.pallas_call(
        functools.partial(prepare_kernel, shards=shards, ff=ff),
        out_shape=(
            jax.ShapeDtypeStruct((width, ff), BF16),
            jax.ShapeDtypeStruct((width, ff), BF16),
            jax.ShapeDtypeStruct((slots, ff), F32),
        ),
        in_specs=vmem(2),
        out_specs=tuple(vmem(3)),
        scratch_shapes=[pltpu.VMEM((slots, width), BF16)],
        compiler_params=params(24),
        cost_estimate=pl.CostEstimate(
            flops=40 * slots * width * ff, bytes_accessed=0, transcendentals=0
        ),
        name="prepare",
    )(recv_cot.reshape(slots * chunks, LANES), weights)

    back = expert(
        recv_rows.reshape(slots * chunks, LANES), full_gate, full_up, down_back, capacity=capacity
    )
    home = exchange(back)

    grad_input, grad_gates = pl.pallas_call(
        functools.partial(combine_kernel, capacity=capacity),
        out_shape=(
            jax.ShapeDtypeStruct((tokens, width), F32),
            jax.ShapeDtypeStruct((top, tokens), BF16),
        ),
        in_specs=vmem(5),
        out_specs=tuple(vmem(2)),
        scratch_shapes=[pltpu.VMEM((slots, width), BF16)],
        compiler_params=params(24),
        name="combine",
    )(home, home[:, each, :], ids, gates, slot_table)
    return grad_input, grad_gates.T


def solution(mesh):
    both = P(("seq", "exp"), None)
    return jax.shard_map(
        local,
        mesh=mesh,
        in_specs=(
            both,
            both,
            both,
            both,
            P(("seq", "exp")),
            P(),
            both,
            both,
            P("exp", "seq", None),
            P("exp", "seq", None),
            P("exp", None, "seq"),
            both,
        ),
        out_specs=(both, both),
        check_vma=False,
    )
```

```python
import functools

import jax
import jax.numpy as jnp
from jax import lax
from jax.experimental import pallas as pl
from jax.experimental.pallas import tpu as pltpu
from jax.sharding import PartitionSpec as P

GROUP = 32
NEG = -1e30
LANES = 128
F32 = jnp.float32
BF16 = jnp.bfloat16
MIB = 1 << 20


def params(mib):
    return pltpu.CompilerParams(vmem_limit_bytes=mib * MIB)


def vmem(count):
    return [pl.BlockSpec(memory_space=pltpu.VMEM)] * count


SMEM = pl.BlockSpec(memory_space=pltpu.SMEM)


def iota(shape, dim):
    return lax.broadcasted_iota(jnp.int32, shape, dim)


def dot(a, b, dims=((1,), (0,))):
    return lax.dot_general(a, b, (dims, ((), ())), preferred_element_type=F32)


def as_bf16(mask):
    return jnp.where(mask, 1.0, 0.0).astype(BF16)


def fold_matrix(slots, chunks):
    rows = slots * chunks
    row, col = iota((rows, rows), 0), iota((rows, rows), 1)
    return as_bf16((row // chunks) + (row % chunks) * slots == col)


def unfold_matrix(slots, chunks):
    rows = slots * chunks
    row, col = iota((rows, rows), 0), iota((rows, rows), 1)
    return as_bf16((col // chunks) + (col % chunks) * slots == row)


BLOCK = 32


def fold_rows(wide, matrix, store):
    chunks = wide.shape[1] // LANES
    size = BLOCK * chunks

    def stacked(b):
        part = wide[b * BLOCK : (b + 1) * BLOCK, :]
        return jnp.concatenate(
            [part[:, c * LANES : (c + 1) * LANES] for c in range(chunks)], axis=0
        )

    for b in range(0, wide.shape[0] // BLOCK, 2):
        two = jnp.concatenate([stacked(b), stacked(b + 1)], axis=1)
        out = dot(matrix, two).astype(BF16)
        store(b * size, out[:, :LANES])
        store((b + 1) * size, out[:, LANES:])


def unfold_rows(load, slots, chunks, matrix, ref):
    size = BLOCK * chunks
    for b in range(0, slots // BLOCK, 2):
        two = jnp.concatenate([load(b * size, size), load((b + 1) * size, size)], axis=1)
        out = dot(matrix, two).astype(BF16)
        for half in range(2):
            for c in range(chunks):
                ref[
                    (b + half) * BLOCK : (b + half + 1) * BLOCK, c * LANES : (c + 1) * LANES
                ] = out[c * BLOCK : (c + 1) * BLOCK, half * LANES : (half + 1) * LANES]


def pack_kernel(lens_ref, key_ref, value_ref, out_ref):
    copies = out_ref.shape[0]
    total = lens_ref[0]
    for i in range(1, lens_ref.shape[0]):
        total = total + lens_ref[i]
    rows = key_ref.shape[0]
    tot = jnp.full((rows, LANES), total.astype(F32), F32).astype(BF16)
    one = jnp.concatenate([key_ref[...], value_ref[...], tot], axis=1)
    out_ref[...] = jnp.broadcast_to(one[None], (copies,) + one.shape)


def segment_kernel(in_ref, out_ref, *, rows):
    count = in_ref.shape[0]
    out_ref[0:count, 0:LANES] = in_ref[:, 0:LANES]
    for i in range(0, count, LANES):
        block = in_ref[i : i + LANES, LANES : 2 * LANES].astype(F32)
        out_ref[i : i + LANES, LANES : 2 * LANES] = block.T.astype(BF16)
    tot = in_ref[:, 2 * LANES :].astype(F32)
    row, lane = iota(tot.shape, 0), iota(tot.shape, 1)
    line = jnp.sum(jnp.where(row == lane * rows, tot, 0.0), axis=0, keepdims=True)
    more = out_ref.shape[0] - count
    line = jnp.broadcast_to(line, (more, LANES))
    out_ref[count:, :] = jnp.concatenate([line, jnp.zeros_like(line)], axis=1).astype(BF16)


def placed(slot_rows, top, slots, values=None):
    tokens = slot_rows.shape[1]
    place = iota((slots, tokens), 0)
    out = jnp.zeros((slots, tokens), F32)
    for k in range(top):
        value = 1.0 if values is None else values[k : k + 1, :]
        out = jnp.where(place == slot_rows[k : k + 1, :], value, out)
    return out.astype(BF16)


def dispatch_kernel(ids_ref, gate_ref, cot_ref, slot_ref, send_ref, *, experts, capacity):
    top, tokens = ids_ref.shape
    ids = ids_ref[...]
    expert = iota((experts, tokens), 0)
    named = jnp.zeros((experts, tokens), F32)
    for k in range(top):
        named = jnp.where(expert == ids[k : k + 1, :], 1.0, named)
    earlier = as_bf16(iota((tokens, tokens), 0) < iota((tokens, tokens), 1))
    before = dot(named.astype(BF16), earlier)
    slot_rows, ranks = [], []
    for k in range(top):
        own = ids[k : k + 1, :]
        rank = jnp.sum(jnp.where(expert == own, before, 0.0), axis=0, keepdims=True)
        rank = rank.astype(jnp.int32)
        ranks.append(rank)
        slot_rows.append(own * capacity + rank)
    both = jnp.concatenate(slot_rows + ranks, axis=0)
    slot_ref[...] = both
    slots = experts * capacity
    spread = placed(both, top, slots, gate_ref[...].astype(F32))
    wide = dot(spread, cot_ref[...]).astype(BF16)
    chunks = cot_ref.shape[1] // LANES

    def store(first, rows):
        send_ref[first : first + rows.shape[0], :] = rows

    fold_rows(wide, fold_matrix(BLOCK, chunks), store)


def attend_kernel(
    place_ref,
    lens_ref,
    kv_hbm,
    query_hbm,
    hidden_hbm,
    proj_hbm,
    slot_hbm,
    send_ref,
    max_ref,
    acc_ref,
    line_buf,
    kv_buf,
    query_ref,
    hidden_ref,
    proj_buf,
    slot_ref,
    line_sem,
    kv_sem,
    other_sem,
    *,
    segments,
    rows,
    pitch,
    top,
    together,
):
    def kv_copy(b):
        at = pl.ds(0, rows)
        return pltpu.make_async_copy(kv_hbm.at[b, at], kv_buf.at[b], kv_sem.at[b])

    def line_copy(b):
        at = pl.ds(rows, pitch - rows)
        return pltpu.make_async_copy(kv_hbm.at[b, at], line_buf.at[b], line_sem.at[b])

    query_copy, hidden_copy, proj_copy, slot_copy = [
        pltpu.make_async_copy(src, dst, other_sem.at[i])
        for i, (src, dst) in enumerate(
            (
                (query_hbm, query_ref),
                (hidden_hbm, hidden_ref),
                (proj_hbm, proj_buf),
                (slot_hbm, slot_ref),
            )
        )
    ]
    for b in range(segments):
        line_copy(b).start()
    query_copy.start()
    for b in range(segments):
        kv_copy(b).start()
    proj_copy.start()
    hidden_copy.start()
    slot_copy.start()
    tokens = query_ref.shape[0]
    heads = query_ref.shape[1] // LANES
    scale = LANES**-0.5 * 1.4426950408889634
    max_ref[...] = jnp.full(max_ref.shape, NEG, F32)
    acc_ref[...] = jnp.zeros(acc_ref.shape, F32)
    extra = acc_ref.shape[1] - LANES
    for b in range(segments):
        line_copy(b).wait()
    seq, exp = place_ref[0], place_ref[1]
    total = jnp.zeros((16, LANES), F32)
    lane = iota((16, LANES), 1)
    for s in range(segments):
        line = line_buf[s, :, 0:LANES].astype(F32)
        take = jnp.logical_or(seq > s, jnp.logical_and(seq == s, lane < exp))
        total = total + jnp.where(take, line, 0.0)
    offset = (jnp.sum(total) * (1.0 / 16.0)).astype(jnp.int32)
    ends = []
    for g in range(lens_ref.shape[0]):
        offset = offset + lens_ref[g]
        ends.append(offset)
    size = together * tokens
    group = (iota((1, size), 1) % tokens) // GROUP
    limits = jnp.zeros((1, size), jnp.int32)
    for g, end in enumerate(ends):
        limits = jnp.where(group == g, end, limits)
    ones = jnp.ones((extra, rows), BF16)

    def block(masked):
        def body(b, carry):
            kv_copy(b).wait()
            keys = kv_buf[b, :, 0:LANES]
            values = jnp.concatenate(
                [kv_buf[b, i : i + LANES, LANES : 2 * LANES] for i in range(0, rows, LANES)],
                axis=1,
            )
            tall = jnp.concatenate([values, ones], axis=0)
            for g in range(heads // together):
                q = jnp.concatenate(
                    [
                        query_ref[:, i * LANES : (i + 1) * LANES]
                        for i in range(g * together, (g + 1) * together)
                    ],
                    axis=0,
                )
                s = dot(keys, q, ((1,), (1,)))
                if masked:
                    s = jnp.where(iota((rows, size), 0) + b * rows < limits, s, NEG)
                old = max_ref[g]
                new = jnp.maximum(old, jnp.max(s, axis=0, keepdims=True))
                max_ref[g] = new
                w = jnp.exp2((s - new) * scale).astype(BF16)
                factor = jnp.exp2((old - new) * scale)
                acc_ref[g] = acc_ref[g] * factor + dot(tall, w)
            return carry

        return body

    full = ends[0] // rows
    last = (ends[-1] + rows - 1) // rows
    query_copy.wait()
    lax.fori_loop(0, full, block(False), 0)
    lax.fori_loop(full, last, block(True), 0)

    def unused(b, carry):
        kv_copy(b).wait()
        return carry

    lax.fori_loop(last, segments, unused, 0)
    attended = []
    for g in range(heads // together):
        acc = acc_ref[g]
        part = (acc[:LANES, :] / acc[LANES : LANES + 1, :]).astype(BF16)
        attended += [part[:, i * tokens : (i + 1) * tokens] for i in range(together)]
    proj_copy.wait()
    hidden_copy.wait()
    slot_copy.wait()
    mixed = hidden_ref[...].astype(F32) + dot(
        jnp.concatenate(attended, axis=0), proj_buf[...], ((0,), (0,))
    )
    chunks = hidden_ref.shape[1] // LANES
    slots = send_ref.shape[0] // chunks
    wide = dot(placed(slot_ref[...], top, slots), mixed.astype(BF16)).astype(BF16)

    def store(first, part):
        send_ref[first : first + part.shape[0], :] = part

    fold_rows(wide, fold_matrix(BLOCK, chunks), store)


def prepare_kernel(cot_ref, weight_ref, back_ref, c_ref, *, shards, ff):
    slots, width = c_ref.shape
    chunks = width // LANES
    unfold_rows(
        lambda f, n: cot_ref[f : f + n, :], slots, chunks, unfold_matrix(BLOCK, chunks), c_ref
    )
    c = c_ref[...]
    step = 256
    for j in range(ff // step):
        w_down = jnp.concatenate(
            [weight_ref[s * ff + j * step : s * ff + (j + 1) * step, :] for s in range(shards)],
            axis=1,
        )
        back_ref[:, j * step : (j + 1) * step] = dot(c, w_down, ((1,), (1,)))


def expert_kernel(
    row_ref,
    weight_ref,
    back_ref,
    out_ref,
    x_ref,
    grad_ref,
    gate_buf,
    up_buf,
    back_buf,
    weight_sem,
    back_sem,
    *,
    capacity,
):
    slots, width = x_ref.shape
    chunks = width // LANES
    shards = weight_ref.shape[0]
    rows = weight_ref.shape[1] // 2
    ff = weight_ref.shape[2]
    others = [pltpu.make_async_copy(back_ref, back_buf, back_sem)]
    for s in range(shards):
        for i, buf in enumerate((gate_buf, up_buf)):
            others.append(
                pltpu.make_async_copy(
                    weight_ref.at[s, pl.ds(i * rows, rows)],
                    buf.at[pl.ds(s * rows, rows)],
                    weight_sem.at[s, i],
                )
            )
    for copy in others:
        copy.start()
    unfold_rows(
        lambda f, n: row_ref[f : f + n, :], slots, chunks, unfold_matrix(BLOCK, chunks), x_ref
    )
    x = x_ref[...]
    for copy in others:
        copy.wait()
    step = 256
    gate_sum = jnp.zeros((slots, 1), F32)
    for j in range(ff // step):
        at = slice(j * step, (j + 1) * step)
        w_gate, w_up = gate_buf[:, at], up_buf[:, at]
        back = back_buf[:, at]
        gate_lin = dot(x, w_gate)
        up_lin = dot(x, w_up)
        sig = 0.5 * jnp.tanh(0.5 * gate_lin) + 0.5
        swish = gate_lin * sig
        up_back = back * swish
        gate_sum = gate_sum + jnp.sum(up_back * up_lin, axis=1, keepdims=True)
        gate_back = back * up_lin * (sig + swish * (1.0 - sig))
        part = dot(gate_back.astype(BF16), w_gate, ((1,), (1,))) + dot(
            up_back.astype(BF16), w_up, ((1,), (1,))
        )
        if j == 0:
            grad_ref[...] = part
        else:
            grad_ref[...] += part
    experts = slots // capacity
    each = capacity * chunks

    def store(first, rows):
        size = rows.shape[0]
        at = first
        while at < first + size:
            e, r = at // each, at % each
            n = min(each - r, first + size - at)
            out_ref[e, r : r + n, :] = rows[at - first : at - first + n, :]
            at += n

    fold_rows(grad_ref[...].astype(BF16), fold_matrix(BLOCK, chunks), store)
    high = gate_sum.astype(BF16)
    low = (gate_sum - high.astype(F32)).astype(BF16)
    slot, lane = iota((slots, LANES), 0), iota((slots, LANES), 1)
    rank = slot % capacity
    spread = jnp.where(rank == lane, high.astype(F32), 0.0) + jnp.where(
        rank + 16 == lane, low.astype(F32), 0.0
    )
    owner = as_bf16(iota((experts, slots), 0) == iota((experts, slots), 1) // capacity)
    lines = dot(owner, spread.astype(BF16)).astype(BF16)
    for e in range(experts):
        out_ref[e, each:, :] = jnp.broadcast_to(
            lines[e : e + 1, :], (out_ref.shape[1] - each, LANES)
        )


def combine_kernel(
    back_ref, line_ref, ids_ref, gate_ref, slot_ref, grad_ref, gates_ref, wide_ref, *, capacity
):
    top, tokens = ids_ref.shape
    slots, width = wide_ref.shape
    chunks = width // LANES
    experts = slots // capacity
    each = capacity * chunks

    def load(first, count):
        parts, at = [], first
        while at < first + count:
            e, r = at // each, at % each
            n = min(each - r, first + count - at)
            parts.append(back_ref[e, r : r + n, :])
            at += n
        return jnp.concatenate(parts, axis=0)

    unfold_rows(load, slots, chunks, unfold_matrix(BLOCK, chunks), wide_ref)
    both = slot_ref[...]
    spread = placed(both, top, slots)
    grad_ref[...] = dot(spread, wide_ref[...], ((0,), (0,)))
    lines = line_ref[...]
    expert = iota((experts, tokens), 0)
    rank = iota((LANES, tokens), 0)
    out = []
    for k in range(top):
        own = as_bf16(expert == ids_ref[k : k + 1, :])
        found = dot(lines, own, ((0,), (0,)))
        mine = both[top + k : top + k + 1, :]
        take = jnp.logical_or(rank == mine, rank == mine + 16)
        value = jnp.sum(jnp.where(take, found, 0.0), axis=0, keepdims=True)
        out.append(value / gate_ref[k : k + 1, :].astype(F32))
    gates_ref[...] = jnp.concatenate(out, axis=0).astype(BF16)


HBM = pl.BlockSpec(memory_space=pltpu.HBM)
TOGETHER = 8


def attend(place, lens, kv, queries, hidden, proj, slot_table, *, rows, slots):
    tokens, width = hidden.shape
    segments, pitch = kv.shape[0], kv.shape[1]
    top = slot_table.shape[0] // 2
    heads, chunks = queries.shape[1] // LANES, width // LANES
    return pl.pallas_call(
        functools.partial(
            attend_kernel, segments=segments, rows=rows, pitch=pitch, top=top, together=TOGETHER
        ),
        out_shape=jax.ShapeDtypeStruct((slots * chunks, LANES), BF16),
        in_specs=[SMEM, SMEM] + [HBM] * 5,
        out_specs=vmem(1)[0],
        scratch_shapes=[
            pltpu.VMEM((heads // TOGETHER, 1, TOGETHER * tokens), F32),
            pltpu.VMEM((heads // TOGETHER, LANES + 16, TOGETHER * tokens), F32),
            pltpu.VMEM((segments, pitch - rows, 2 * LANES), BF16),
            pltpu.VMEM((segments, rows, 2 * LANES), BF16),
            pltpu.VMEM(queries.shape, BF16),
            pltpu.VMEM(hidden.shape, BF16),
            pltpu.VMEM(proj.shape, BF16),
            pltpu.VMEM(slot_table.shape, jnp.int32),
            pltpu.SemaphoreType.DMA((segments,)),
            pltpu.SemaphoreType.DMA((segments,)),
            pltpu.SemaphoreType.DMA((4,)),
        ],
        compiler_params=params(58),
        cost_estimate=pl.CostEstimate(flops=0, bytes_accessed=0, transcendentals=0),
        name="attend",
    )(place, lens, kv, queries, hidden, proj, slot_table)


def expert(rows, weights, back, *, capacity):
    slots, (shards, pair, ff) = back.shape[0], weights.shape
    width = shards * pair // 2
    chunks = width // LANES
    return pl.pallas_call(
        functools.partial(expert_kernel, capacity=capacity),
        out_shape=jax.ShapeDtypeStruct((slots // capacity, capacity * chunks + 8, LANES), BF16),
        in_specs=vmem(1) + [HBM] * 2,
        out_specs=vmem(1)[0],
        scratch_shapes=[
            pltpu.VMEM((slots, width), BF16),
            pltpu.VMEM((slots, width), F32),
            pltpu.VMEM((width, ff), BF16),
            pltpu.VMEM((width, ff), BF16),
            pltpu.VMEM(back.shape, F32),
            pltpu.SemaphoreType.DMA((shards, 2)),
            pltpu.SemaphoreType.DMA(()),
        ],
        compiler_params=params(50),
        name="expert",
    )(rows, weights, back)


def exchange(rows):
    return lax.all_to_all(rows, "exp", split_axis=0, concat_axis=0, tiled=True)


def local(
    hidden,
    queries,
    thinker_keys,
    thinker_values,
    thinker_lengths,
    out_proj,
    expert_ids,
    gate_values,
    w_gate,
    w_up,
    w_down,
    cotangent,
):
    tokens, width = hidden.shape
    top = expert_ids.shape[1]
    experts, shards = lax.axis_size("exp"), lax.axis_size("seq")
    capacity = tokens * top * 5 // (4 * experts)
    slots = experts * capacity
    chunks = width // LANES
    each = capacity * chunks
    ff = w_gate.shape[2]
    own_rows = thinker_keys.shape[0]
    rows = experts * own_rows
    pitch = rows + 16
    place = jnp.stack([lax.axis_index("seq"), lax.axis_index("exp")]).astype(jnp.int32)
    ids, gates = expert_ids.T, gate_values.T

    packed = pl.pallas_call(
        pack_kernel,
        out_shape=jax.ShapeDtypeStruct((experts, own_rows, 3 * LANES), BF16),
        in_specs=[SMEM] + vmem(2),
        out_specs=vmem(1)[0],
        compiler_params=params(16),
        name="pack",
    )(thinker_lengths, thinker_keys, thinker_values)
    kv_rows = exchange(packed)

    slot_table, send_cot = pl.pallas_call(
        functools.partial(dispatch_kernel, experts=experts, capacity=capacity),
        out_shape=(
            jax.ShapeDtypeStruct((2 * top, tokens), jnp.int32),
            jax.ShapeDtypeStruct((slots * chunks, LANES), BF16),
        ),
        in_specs=vmem(3),
        out_specs=tuple(vmem(2)),
        compiler_params=params(24),
        name="dispatch",
    )(ids, gates, cotangent)

    segment = pl.pallas_call(
        functools.partial(segment_kernel, rows=own_rows),
        out_shape=jax.ShapeDtypeStruct((pitch, 2 * LANES), BF16),
        in_specs=vmem(1),
        out_specs=vmem(1)[0],
        compiler_params=params(16),
        name="segment",
    )(kv_rows.reshape(rows, 3 * LANES))
    down = lax.all_gather(w_down[0], "seq", axis=0, tiled=True)
    shard = jnp.concatenate([w_gate[0], w_up[0]], axis=0)
    segment, send_cot, shard, down = lax.optimization_barrier((segment, send_cot, shard, down))
    kv_all = lax.all_gather(segment, "seq", axis=0, tiled=True)
    recv_cot = exchange(send_cot.reshape(experts, each, LANES))
    weights = lax.all_gather(shard, "seq", axis=0, tiled=False)

    send_rows = attend(
        place,
        thinker_lengths,
        kv_all.reshape(shards, pitch, 2 * LANES),
        queries,
        hidden,
        out_proj,
        slot_table,
        rows=rows,
        slots=slots,
    )
    send_rows, recv_cot = lax.optimization_barrier((send_rows, recv_cot))
    recv_rows = exchange(send_rows.reshape(experts, each, LANES))
    down_back = pl.pallas_call(
        functools.partial(prepare_kernel, shards=shards, ff=ff),
        out_shape=jax.ShapeDtypeStruct((slots, ff), F32),
        in_specs=vmem(2),
        out_specs=vmem(1)[0],
        scratch_shapes=[pltpu.VMEM((slots, width), BF16)],
        compiler_params=params(24),
        cost_estimate=pl.CostEstimate(
            flops=40 * slots * width * ff, bytes_accessed=0, transcendentals=0
        ),
        name="prepare",
    )(recv_cot.reshape(slots * chunks, LANES), down)
    back = expert(
        recv_rows.reshape(slots * chunks, LANES), weights, down_back, capacity=capacity
    )
    home = exchange(back)

    grad_input, grad_gates = pl.pallas_call(
        functools.partial(combine_kernel, capacity=capacity),
        out_shape=(
            jax.ShapeDtypeStruct((tokens, width), F32),
            jax.ShapeDtypeStruct((top, tokens), BF16),
        ),
        in_specs=vmem(5),
        out_specs=tuple(vmem(2)),
        scratch_shapes=[pltpu.VMEM((slots, width), BF16)],
        compiler_params=params(24),
        name="combine",
    )(home, home[:, each, :], ids, gates, slot_table)
    return grad_input, grad_gates.T


def solution(mesh):
    both = P(("seq", "exp"), None)
    return jax.shard_map(
        local,
        mesh=mesh,
        in_specs=(
            both,
            both,
            both,
            both,
            P(("seq", "exp")),
            P(),
            both,
            both,
            P("exp", "seq", None),
            P("exp", "seq", None),
            P("exp", None, "seq"),
            both,
        ),
        out_specs=(both, both),
        check_vma=False,
    )
```

```python
import functools

import jax
import jax.numpy as jnp
from jax import lax
from jax.experimental import pallas as pl
from jax.experimental.pallas import tpu as pltpu
from jax.sharding import PartitionSpec as P

GROUP = 32
NEG = -1e30
LANES = 128
F32 = jnp.float32
BF16 = jnp.bfloat16
MIB = 1 << 20


def params(mib):
    return pltpu.CompilerParams(vmem_limit_bytes=mib * MIB)


def vmem(count):
    return [pl.BlockSpec(memory_space=pltpu.VMEM)] * count


SMEM = pl.BlockSpec(memory_space=pltpu.SMEM)


def iota(shape, dim):
    return lax.broadcasted_iota(jnp.int32, shape, dim)


def dot(a, b, dims=((1,), (0,))):
    return lax.dot_general(a, b, (dims, ((), ())), preferred_element_type=F32)


def as_bf16(mask):
    return jnp.where(mask, 1.0, 0.0).astype(BF16)


def fold_matrix(slots, chunks):
    rows = slots * chunks
    row, col = iota((rows, rows), 0), iota((rows, rows), 1)
    return as_bf16((row // chunks) + (row % chunks) * slots == col)


def unfold_matrix(slots, chunks):
    rows = slots * chunks
    row, col = iota((rows, rows), 0), iota((rows, rows), 1)
    return as_bf16((col // chunks) + (col % chunks) * slots == row)


BLOCK = 32


def fold_rows(wide, matrix, store):
    chunks = wide.shape[1] // LANES
    size = BLOCK * chunks

    def stacked(b):
        part = wide[b * BLOCK : (b + 1) * BLOCK, :]
        return jnp.concatenate(
            [part[:, c * LANES : (c + 1) * LANES] for c in range(chunks)], axis=0
        )

    for b in range(0, wide.shape[0] // BLOCK, 2):
        two = jnp.concatenate([stacked(b), stacked(b + 1)], axis=1)
        out = dot(matrix, two).astype(BF16)
        store(b * size, out[:, :LANES])
        store((b + 1) * size, out[:, LANES:])


def unfold_rows(load, slots, chunks, matrix, ref):
    size = BLOCK * chunks
    for b in range(0, slots // BLOCK, 2):
        two = jnp.concatenate([load(b * size, size), load((b + 1) * size, size)], axis=1)
        out = dot(matrix, two).astype(BF16)
        for half in range(2):
            for c in range(chunks):
                ref[
                    (b + half) * BLOCK : (b + half + 1) * BLOCK, c * LANES : (c + 1) * LANES
                ] = out[c * BLOCK : (c + 1) * BLOCK, half * LANES : (half + 1) * LANES]


def pack_kernel(lens_ref, key_hbm, value_hbm, out_ref, key_ref, value_ref, sem):
    copies = [
        pltpu.make_async_copy(key_hbm, key_ref, sem.at[0]),
        pltpu.make_async_copy(value_hbm, value_ref, sem.at[1]),
    ]
    for copy in copies:
        copy.start()
    copies_out = out_ref.shape[0]
    total = lens_ref[0]
    for i in range(1, lens_ref.shape[0]):
        total = total + lens_ref[i]
    rows = key_ref.shape[0]
    tot = jnp.full((rows, LANES), total.astype(F32), F32).astype(BF16)
    for copy in copies:
        copy.wait()
    one = jnp.concatenate([key_ref[...], value_ref[...], tot], axis=1)
    out_ref[...] = jnp.broadcast_to(one[None], (copies_out,) + one.shape)


def segment_kernel(in_ref, out_ref, *, rows):
    count = in_ref.shape[0]
    out_ref[0:count, 0:LANES] = in_ref[:, 0:LANES]
    for i in range(0, count, LANES):
        block = in_ref[i : i + LANES, LANES : 2 * LANES].astype(F32)
        out_ref[i : i + LANES, LANES : 2 * LANES] = block.T.astype(BF16)
    tot = in_ref[:, 2 * LANES :].astype(F32)
    row, lane = iota(tot.shape, 0), iota(tot.shape, 1)
    line = jnp.sum(jnp.where(row == lane * rows, tot, 0.0), axis=0, keepdims=True)
    more = out_ref.shape[0] - count
    line = jnp.broadcast_to(line, (more, LANES))
    out_ref[count:, :] = jnp.concatenate([line, jnp.zeros_like(line)], axis=1).astype(BF16)


def placed(slot_rows, top, slots, values=None):
    tokens = slot_rows.shape[1]
    place = iota((slots, tokens), 0)
    out = jnp.zeros((slots, tokens), F32)
    for k in range(top):
        value = 1.0 if values is None else values[k : k + 1, :]
        out = jnp.where(place == slot_rows[k : k + 1, :], value, out)
    return out.astype(BF16)


def dispatch_kernel(ids_ref, gate_ref, cot_ref, slot_ref, send_ref, *, experts, capacity):
    top, tokens = ids_ref.shape
    ids = ids_ref[...]
    expert = iota((experts, tokens), 0)
    named = jnp.zeros((experts, tokens), F32)
    for k in range(top):
        named = jnp.where(expert == ids[k : k + 1, :], 1.0, named)
    earlier = as_bf16(iota((tokens, tokens), 0) < iota((tokens, tokens), 1))
    before = dot(named.astype(BF16), earlier)
    slot_rows, ranks = [], []
    for k in range(top):
        own = ids[k : k + 1, :]
        rank = jnp.sum(jnp.where(expert == own, before, 0.0), axis=0, keepdims=True)
        rank = rank.astype(jnp.int32)
        ranks.append(rank)
        slot_rows.append(own * capacity + rank)
    both = jnp.concatenate(slot_rows + ranks, axis=0)
    slot_ref[...] = both
    slots = experts * capacity
    spread = placed(both, top, slots, gate_ref[...].astype(F32))
    wide = dot(spread, cot_ref[...]).astype(BF16)
    chunks = cot_ref.shape[1] // LANES

    def store(first, rows):
        send_ref[first : first + rows.shape[0], :] = rows

    fold_rows(wide, fold_matrix(BLOCK, chunks), store)


def attend_kernel(
    place_ref,
    lens_ref,
    kv_hbm,
    query_hbm,
    hidden_hbm,
    proj_hbm,
    slot_hbm,
    send_ref,
    max_ref,
    acc_ref,
    line_buf,
    kv_buf,
    query_ref,
    hidden_ref,
    proj_buf,
    slot_ref,
    line_sem,
    kv_sem,
    other_sem,
    *,
    segments,
    rows,
    pitch,
    top,
    together,
):
    def kv_copy(b):
        at = pl.ds(0, rows)
        return pltpu.make_async_copy(kv_hbm.at[b, at], kv_buf.at[b], kv_sem.at[b])

    def line_copy(b):
        at = pl.ds(rows, pitch - rows)
        return pltpu.make_async_copy(kv_hbm.at[b, at], line_buf.at[b], line_sem.at[b])

    query_copy, hidden_copy, proj_copy, slot_copy = [
        pltpu.make_async_copy(src, dst, other_sem.at[i])
        for i, (src, dst) in enumerate(
            (
                (query_hbm, query_ref),
                (hidden_hbm, hidden_ref),
                (proj_hbm, proj_buf),
                (slot_hbm, slot_ref),
            )
        )
    ]
    for b in range(segments):
        line_copy(b).start()
    query_copy.start()
    for b in range(segments):
        kv_copy(b).start()
    proj_copy.start()
    hidden_copy.start()
    slot_copy.start()
    tokens = query_ref.shape[0]
    heads = query_ref.shape[1] // LANES
    scale = LANES**-0.5 * 1.4426950408889634
    max_ref[...] = jnp.full(max_ref.shape, NEG, F32)
    acc_ref[...] = jnp.zeros(acc_ref.shape, F32)
    extra = acc_ref.shape[1] - LANES
    for b in range(segments):
        line_copy(b).wait()
    seq, exp = place_ref[0], place_ref[1]
    total = jnp.zeros((16, LANES), F32)
    lane = iota((16, LANES), 1)
    for s in range(segments):
        line = line_buf[s, :, 0:LANES].astype(F32)
        take = jnp.logical_or(seq > s, jnp.logical_and(seq == s, lane < exp))
        total = total + jnp.where(take, line, 0.0)
    offset = (jnp.sum(total) * (1.0 / 16.0)).astype(jnp.int32)
    ends = []
    for g in range(lens_ref.shape[0]):
        offset = offset + lens_ref[g]
        ends.append(offset)
    size = together * tokens
    group = (iota((1, size), 1) % tokens) // GROUP
    limits = jnp.zeros((1, size), jnp.int32)
    for g, end in enumerate(ends):
        limits = jnp.where(group == g, end, limits)
    ones = jnp.ones((extra, rows), BF16)

    def block(masked):
        def body(b, carry):
            kv_copy(b).wait()
            keys = kv_buf[b, :, 0:LANES]
            values = jnp.concatenate(
                [kv_buf[b, i : i + LANES, LANES : 2 * LANES] for i in range(0, rows, LANES)],
                axis=1,
            )
            tall = jnp.concatenate([values, ones], axis=0)
            for g in range(heads // together):
                q = jnp.concatenate(
                    [
                        query_ref[:, i * LANES : (i + 1) * LANES]
                        for i in range(g * together, (g + 1) * together)
                    ],
                    axis=0,
                )
                s = dot(keys, q, ((1,), (1,)))
                if masked:
                    s = jnp.where(iota((rows, size), 0) + b * rows < limits, s, NEG)
                old = max_ref[g]
                new = jnp.maximum(old, jnp.max(s, axis=0, keepdims=True))
                max_ref[g] = new
                w = jnp.exp2((s - new) * scale).astype(BF16)
                factor = jnp.exp2((old - new) * scale)
                acc_ref[g] = acc_ref[g] * factor + dot(tall, w)
            return carry

        return body

    full = ends[0] // rows
    last = (ends[-1] + rows - 1) // rows
    query_copy.wait()
    lax.fori_loop(0, full, block(False), 0)
    lax.fori_loop(full, last, block(True), 0)

    def unused(b, carry):
        kv_copy(b).wait()
        return carry

    lax.fori_loop(last, segments, unused, 0)
    attended = []
    for g in range(heads // together):
        acc = acc_ref[g]
        part = (acc[:LANES, :] / acc[LANES : LANES + 1, :]).astype(BF16)
        attended += [part[:, i * tokens : (i + 1) * tokens] for i in range(together)]
    proj_copy.wait()
    hidden_copy.wait()
    slot_copy.wait()
    mixed = hidden_ref[...].astype(F32) + dot(
        jnp.concatenate(attended, axis=0), proj_buf[...], ((0,), (0,))
    )
    chunks = hidden_ref.shape[1] // LANES
    slots = send_ref.shape[0] // chunks
    wide = dot(placed(slot_ref[...], top, slots), mixed.astype(BF16)).astype(BF16)

    def store(first, part):
        send_ref[first : first + part.shape[0], :] = part

    fold_rows(wide, fold_matrix(BLOCK, chunks), store)


def prepare_kernel(cot_ref, weight_ref, back_ref, c_ref, down_buf, down_sem):
    slots, width = c_ref.shape
    chunks = width // LANES
    shards, _, ff = down_buf.shape
    copies = [
        pltpu.make_async_copy(
            weight_ref.at[s, pl.ds(2 * LANES, LANES)], down_buf.at[s], down_sem.at[s]
        )
        for s in range(shards)
    ]
    for copy in copies:
        copy.start()
    unfold_rows(
        lambda f, n: cot_ref[f : f + n, :], slots, chunks, unfold_matrix(BLOCK, chunks), c_ref
    )
    c = c_ref[...]
    for copy in copies:
        copy.wait()
    step = 256
    for j in range(0, ff, step):
        w_down = jnp.concatenate(
            [
                jnp.concatenate(
                    [down_buf[s, :, i : i + LANES] for i in range(j, j + step, LANES)], axis=0
                )
                for s in range(shards)
            ],
            axis=1,
        )
        back_ref[:, j : j + step] = dot(c, w_down, ((1,), (1,)))


def expert_kernel(
    row_ref,
    weight_ref,
    back_ref,
    out_ref,
    x_ref,
    grad_ref,
    gate_buf,
    up_buf,
    back_buf,
    weight_sem,
    back_sem,
    *,
    capacity,
):
    slots, width = x_ref.shape
    chunks = width // LANES
    shards = weight_ref.shape[0]
    rows = gate_buf.shape[0] // shards
    ff = weight_ref.shape[2]
    others = [pltpu.make_async_copy(back_ref, back_buf, back_sem)]
    for s in range(shards):
        for i, buf in enumerate((gate_buf, up_buf)):
            others.append(
                pltpu.make_async_copy(
                    weight_ref.at[s, pl.ds(i * rows, rows)],
                    buf.at[pl.ds(s * rows, rows)],
                    weight_sem.at[s, i],
                )
            )
    for copy in others:
        copy.start()
    unfold_rows(
        lambda f, n: row_ref[f : f + n, :], slots, chunks, unfold_matrix(BLOCK, chunks), x_ref
    )
    x = x_ref[...]
    for copy in others:
        copy.wait()
    step = 256
    gate_sum = jnp.zeros((slots, 1), F32)
    for j in range(ff // step):
        at = slice(j * step, (j + 1) * step)
        w_gate, w_up = gate_buf[:, at], up_buf[:, at]
        back = back_buf[:, at]
        gate_lin = dot(x, w_gate)
        up_lin = dot(x, w_up)
        sig = 0.5 * jnp.tanh(0.5 * gate_lin) + 0.5
        swish = gate_lin * sig
        up_back = back * swish
        gate_sum = gate_sum + jnp.sum(up_back * up_lin, axis=1, keepdims=True)
        gate_back = back * up_lin * (sig + swish * (1.0 - sig))
        part = dot(gate_back.astype(BF16), w_gate, ((1,), (1,))) + dot(
            up_back.astype(BF16), w_up, ((1,), (1,))
        )
        if j == 0:
            grad_ref[...] = part
        else:
            grad_ref[...] += part
    experts = slots // capacity
    each = capacity * chunks

    def store(first, rows):
        size = rows.shape[0]
        at = first
        while at < first + size:
            e, r = at // each, at % each
            n = min(each - r, first + size - at)
            out_ref[e, r : r + n, :] = rows[at - first : at - first + n, :]
            at += n

    fold_rows(grad_ref[...].astype(BF16), fold_matrix(BLOCK, chunks), store)
    high = gate_sum.astype(BF16)
    low = (gate_sum - high.astype(F32)).astype(BF16)
    slot, lane = iota((slots, LANES), 0), iota((slots, LANES), 1)
    rank = slot % capacity
    spread = jnp.where(rank == lane, high.astype(F32), 0.0) + jnp.where(
        rank + 16 == lane, low.astype(F32), 0.0
    )
    owner = as_bf16(iota((experts, slots), 0) == iota((experts, slots), 1) // capacity)
    lines = dot(owner, spread.astype(BF16)).astype(BF16)
    for e in range(experts):
        out_ref[e, each:, :] = jnp.broadcast_to(
            lines[e : e + 1, :], (out_ref.shape[1] - each, LANES)
        )


def combine_kernel(
    back_ref, line_ref, ids_ref, gate_ref, slot_ref, grad_ref, gates_ref, wide_ref, *, capacity
):
    top, tokens = ids_ref.shape
    slots, width = wide_ref.shape
    chunks = width // LANES
    experts = slots // capacity
    each = capacity * chunks

    def load(first, count):
        parts, at = [], first
        while at < first + count:
            e, r = at // each, at % each
            n = min(each - r, first + count - at)
            parts.append(back_ref[e, r : r + n, :])
            at += n
        return jnp.concatenate(parts, axis=0)

    unfold_rows(load, slots, chunks, unfold_matrix(BLOCK, chunks), wide_ref)
    both = slot_ref[...]
    spread = placed(both, top, slots)
    grad_ref[...] = dot(spread, wide_ref[...], ((0,), (0,)))
    lines = line_ref[...]
    expert = iota((experts, tokens), 0)
    rank = iota((LANES, tokens), 0)
    out = []
    for k in range(top):
        own = as_bf16(expert == ids_ref[k : k + 1, :])
        found = dot(lines, own, ((0,), (0,)))
        mine = both[top + k : top + k + 1, :]
        take = jnp.logical_or(rank == mine, rank == mine + 16)
        value = jnp.sum(jnp.where(take, found, 0.0), axis=0, keepdims=True)
        out.append(value / gate_ref[k : k + 1, :].astype(F32))
    gates_ref[...] = jnp.concatenate(out, axis=0).astype(BF16)


HBM = pl.BlockSpec(memory_space=pltpu.HBM)
TOGETHER = 8


def attend(place, lens, kv, queries, hidden, proj, slot_table, *, rows, slots):
    tokens, width = hidden.shape
    segments, pitch = kv.shape[0], kv.shape[1]
    top = slot_table.shape[0] // 2
    heads, chunks = queries.shape[1] // LANES, width // LANES
    return pl.pallas_call(
        functools.partial(
            attend_kernel, segments=segments, rows=rows, pitch=pitch, top=top, together=TOGETHER
        ),
        out_shape=jax.ShapeDtypeStruct((slots * chunks, LANES), BF16),
        in_specs=[SMEM, SMEM] + [HBM] * 5,
        out_specs=vmem(1)[0],
        scratch_shapes=[
            pltpu.VMEM((heads // TOGETHER, 1, TOGETHER * tokens), F32),
            pltpu.VMEM((heads // TOGETHER, LANES + 16, TOGETHER * tokens), F32),
            pltpu.VMEM((segments, pitch - rows, 2 * LANES), BF16),
            pltpu.VMEM((segments, rows, 2 * LANES), BF16),
            pltpu.VMEM(queries.shape, BF16),
            pltpu.VMEM(hidden.shape, BF16),
            pltpu.VMEM(proj.shape, BF16),
            pltpu.VMEM(slot_table.shape, jnp.int32),
            pltpu.SemaphoreType.DMA((segments,)),
            pltpu.SemaphoreType.DMA((segments,)),
            pltpu.SemaphoreType.DMA((4,)),
        ],
        compiler_params=params(58),
        cost_estimate=pl.CostEstimate(flops=0, bytes_accessed=0, transcendentals=0),
        name="attend",
    )(place, lens, kv, queries, hidden, proj, slot_table)


def expert(rows, weights, back, *, capacity):
    slots, (shards, _, ff) = back.shape[0], weights.shape
    width = shards * LANES
    chunks = width // LANES
    return pl.pallas_call(
        functools.partial(expert_kernel, capacity=capacity),
        out_shape=jax.ShapeDtypeStruct((slots // capacity, capacity * chunks + 8, LANES), BF16),
        in_specs=vmem(1) + [HBM] * 2,
        out_specs=vmem(1)[0],
        scratch_shapes=[
            pltpu.VMEM((slots, width), BF16),
            pltpu.VMEM((slots, width), F32),
            pltpu.VMEM((width, ff), BF16),
            pltpu.VMEM((width, ff), BF16),
            pltpu.VMEM(back.shape, F32),
            pltpu.SemaphoreType.DMA((shards, 2)),
            pltpu.SemaphoreType.DMA(()),
        ],
        compiler_params=params(50),
        name="expert",
    )(rows, weights, back)


def exchange(rows):
    return lax.all_to_all(rows, "exp", split_axis=0, concat_axis=0, tiled=True)


def local(
    hidden,
    queries,
    thinker_keys,
    thinker_values,
    thinker_lengths,
    out_proj,
    expert_ids,
    gate_values,
    w_gate,
    w_up,
    w_down,
    cotangent,
):
    tokens, width = hidden.shape
    top = expert_ids.shape[1]
    experts, shards = lax.axis_size("exp"), lax.axis_size("seq")
    capacity = tokens * top * 5 // (4 * experts)
    slots = experts * capacity
    chunks = width // LANES
    each = capacity * chunks
    ff = w_gate.shape[2]
    own_rows = thinker_keys.shape[0]
    rows = experts * own_rows
    pitch = rows + 16
    place = jnp.stack([lax.axis_index("seq"), lax.axis_index("exp")]).astype(jnp.int32)
    ids, gates = expert_ids.T, gate_values.T

    packed = pl.pallas_call(
        pack_kernel,
        out_shape=jax.ShapeDtypeStruct((experts, own_rows, 3 * LANES), BF16),
        in_specs=[SMEM, HBM, HBM],
        out_specs=vmem(1)[0],
        scratch_shapes=[
            pltpu.VMEM(thinker_keys.shape, BF16),
            pltpu.VMEM(thinker_values.shape, BF16),
            pltpu.SemaphoreType.DMA((2,)),
        ],
        compiler_params=params(58),
        name="pack",
    )(thinker_lengths, thinker_keys, thinker_values)
    kv_rows = exchange(packed)

    slot_table, send_cot = pl.pallas_call(
        functools.partial(dispatch_kernel, experts=experts, capacity=capacity),
        out_shape=(
            jax.ShapeDtypeStruct((2 * top, tokens), jnp.int32),
            jax.ShapeDtypeStruct((slots * chunks, LANES), BF16),
        ),
        in_specs=vmem(3),
        out_specs=tuple(vmem(2)),
        compiler_params=params(24),
        name="dispatch",
    )(ids, gates, cotangent)

    segment = pl.pallas_call(
        functools.partial(segment_kernel, rows=own_rows),
        out_shape=jax.ShapeDtypeStruct((pitch, 2 * LANES), BF16),
        in_specs=vmem(1),
        out_specs=vmem(1)[0],
        compiler_params=params(16),
        name="segment",
    )(kv_rows.reshape(rows, 3 * LANES))
    lower = jnp.concatenate(
        [w_down[0][i * LANES : (i + 1) * LANES, :] for i in range(ff // LANES)], axis=1
    )
    shard = jnp.concatenate([w_gate[0], w_up[0], lower], axis=0)
    segment, send_cot, shard = lax.optimization_barrier((segment, send_cot, shard))
    kv_all = lax.all_gather(segment, "seq", axis=0, tiled=True)
    recv_cot = exchange(send_cot.reshape(experts, each, LANES))
    weights = lax.all_gather(shard, "seq", axis=0, tiled=False)

    send_rows = attend(
        place,
        thinker_lengths,
        kv_all.reshape(shards, pitch, 2 * LANES),
        queries,
        hidden,
        out_proj,
        slot_table,
        rows=rows,
        slots=slots,
    )
    send_rows, recv_cot = lax.optimization_barrier((send_rows, recv_cot))
    recv_rows = exchange(send_rows.reshape(experts, each, LANES))
    down_back = pl.pallas_call(
        prepare_kernel,
        out_shape=jax.ShapeDtypeStruct((slots, ff), F32),
        in_specs=[vmem(1)[0], HBM],
        out_specs=vmem(1)[0],
        scratch_shapes=[
            pltpu.VMEM((slots, width), BF16),
            pltpu.VMEM((shards, LANES, ff), BF16),
            pltpu.SemaphoreType.DMA((shards,)),
        ],
        compiler_params=params(50),
        cost_estimate=pl.CostEstimate(
            flops=40 * slots * width * ff, bytes_accessed=0, transcendentals=0
        ),
        name="prepare",
    )(recv_cot.reshape(slots * chunks, LANES), weights)
    back = expert(
        recv_rows.reshape(slots * chunks, LANES), weights, down_back, capacity=capacity
    )
    home = exchange(back)

    grad_input, grad_gates = pl.pallas_call(
        functools.partial(combine_kernel, capacity=capacity),
        out_shape=(
            jax.ShapeDtypeStruct((tokens, width), F32),
            jax.ShapeDtypeStruct((top, tokens), BF16),
        ),
        in_specs=vmem(5),
        out_specs=tuple(vmem(2)),
        scratch_shapes=[pltpu.VMEM((slots, width), BF16)],
        compiler_params=params(24),
        name="combine",
    )(home, home[:, each, :], ids, gates, slot_table)
    return grad_input, grad_gates.T


def solution(mesh):
    both = P(("seq", "exp"), None)
    return jax.shard_map(
        local,
        mesh=mesh,
        in_specs=(
            both,
            both,
            both,
            both,
            P(("seq", "exp")),
            P(),
            both,
            both,
            P("exp", "seq", None),
            P("exp", "seq", None),
            P("exp", None, "seq"),
            both,
        ),
        out_specs=(both, both),
        check_vma=False,
    )
```

```python
import functools

import jax
import jax.numpy as jnp
from jax import lax
from jax.experimental import pallas as pl
from jax.experimental.pallas import tpu as pltpu
from jax.sharding import PartitionSpec as P

GROUP = 32
NEG = -1e30
LANES = 128
F32 = jnp.float32
BF16 = jnp.bfloat16
MIB = 1 << 20


def params(mib):
    return pltpu.CompilerParams(vmem_limit_bytes=mib * MIB)


def vmem(count):
    return [pl.BlockSpec(memory_space=pltpu.VMEM)] * count


SMEM = pl.BlockSpec(memory_space=pltpu.SMEM)


def iota(shape, dim):
    return lax.broadcasted_iota(jnp.int32, shape, dim)


def dot(a, b, dims=((1,), (0,))):
    return lax.dot_general(a, b, (dims, ((), ())), preferred_element_type=F32)


def as_bf16(mask):
    return jnp.where(mask, 1.0, 0.0).astype(BF16)


def fold_matrix(slots, chunks):
    rows = slots * chunks
    row, col = iota((rows, rows), 0), iota((rows, rows), 1)
    return as_bf16((row // chunks) + (row % chunks) * slots == col)


def unfold_matrix(slots, chunks):
    rows = slots * chunks
    row, col = iota((rows, rows), 0), iota((rows, rows), 1)
    return as_bf16((col // chunks) + (col % chunks) * slots == row)


BLOCK = 32


def fold_rows(wide, matrix, store):
    chunks = wide.shape[1] // LANES
    size = BLOCK * chunks

    def stacked(b):
        part = wide[b * BLOCK : (b + 1) * BLOCK, :]
        return jnp.concatenate(
            [part[:, c * LANES : (c + 1) * LANES] for c in range(chunks)], axis=0
        )

    for b in range(0, wide.shape[0] // BLOCK, 2):
        two = jnp.concatenate([stacked(b), stacked(b + 1)], axis=1)
        out = dot(matrix, two).astype(BF16)
        store(b * size, out[:, :LANES])
        store((b + 1) * size, out[:, LANES:])


def unfold_rows(load, slots, chunks, matrix, ref):
    size = BLOCK * chunks
    for b in range(0, slots // BLOCK, 2):
        two = jnp.concatenate([load(b * size, size), load((b + 1) * size, size)], axis=1)
        out = dot(matrix, two).astype(BF16)
        for half in range(2):
            for c in range(chunks):
                ref[
                    (b + half) * BLOCK : (b + half + 1) * BLOCK, c * LANES : (c + 1) * LANES
                ] = out[c * BLOCK : (c + 1) * BLOCK, half * LANES : (half + 1) * LANES]


def pack_kernel(lens_ref, key_hbm, value_hbm, out_ref, key_ref, value_ref, sem):
    copies = [
        pltpu.make_async_copy(key_hbm, key_ref, sem.at[0]),
        pltpu.make_async_copy(value_hbm, value_ref, sem.at[1]),
    ]
    for copy in copies:
        copy.start()
    copies_out = out_ref.shape[0]
    total = lens_ref[0]
    for i in range(1, lens_ref.shape[0]):
        total = total + lens_ref[i]
    rows = key_ref.shape[0]
    tot = jnp.full((rows, LANES), total.astype(F32), F32).astype(BF16)
    for copy in copies:
        copy.wait()
    one = jnp.concatenate([key_ref[...], value_ref[...], tot], axis=1)
    out_ref[...] = jnp.broadcast_to(one[None], (copies_out,) + one.shape)


def segment_kernel(in_ref, out_ref, *, rows):
    count = in_ref.shape[0]
    out_ref[0:count, 0:LANES] = in_ref[:, 0:LANES]
    for i in range(0, count, LANES):
        block = in_ref[i : i + LANES, LANES : 2 * LANES].astype(F32)
        out_ref[i : i + LANES, LANES : 2 * LANES] = block.T.astype(BF16)
    tot = in_ref[:, 2 * LANES :].astype(F32)
    row, lane = iota(tot.shape, 0), iota(tot.shape, 1)
    line = jnp.sum(jnp.where(row == lane * rows, tot, 0.0), axis=0, keepdims=True)
    more = out_ref.shape[0] - count
    line = jnp.broadcast_to(line, (more, LANES))
    out_ref[count:, :] = jnp.concatenate([line, jnp.zeros_like(line)], axis=1).astype(BF16)


def placed(slot_rows, top, slots, values=None):
    tokens = slot_rows.shape[1]
    place = iota((slots, tokens), 0)
    out = jnp.zeros((slots, tokens), F32)
    for k in range(top):
        value = 1.0 if values is None else values[k : k + 1, :]
        out = jnp.where(place == slot_rows[k : k + 1, :], value, out)
    return out.astype(BF16)


def dispatch_kernel(ids_ref, gate_ref, cot_ref, slot_ref, send_ref, *, experts, capacity):
    top, tokens = ids_ref.shape
    ids = ids_ref[...]
    expert = iota((experts, tokens), 0)
    named = jnp.zeros((experts, tokens), F32)
    for k in range(top):
        named = jnp.where(expert == ids[k : k + 1, :], 1.0, named)
    earlier = as_bf16(iota((tokens, tokens), 0) < iota((tokens, tokens), 1))
    before = dot(named.astype(BF16), earlier)
    slot_rows, ranks = [], []
    for k in range(top):
        own = ids[k : k + 1, :]
        rank = jnp.sum(jnp.where(expert == own, before, 0.0), axis=0, keepdims=True)
        rank = rank.astype(jnp.int32)
        ranks.append(rank)
        slot_rows.append(own * capacity + rank)
    both = jnp.concatenate(slot_rows + ranks, axis=0)
    slot_ref[...] = both
    slots = experts * capacity
    spread = placed(both, top, slots, gate_ref[...].astype(F32))
    wide = dot(spread, cot_ref[...]).astype(BF16)
    chunks = cot_ref.shape[1] // LANES

    def store(first, rows):
        send_ref[first : first + rows.shape[0], :] = rows

    fold_rows(wide, fold_matrix(BLOCK, chunks), store)


def attend_kernel(
    place_ref,
    lens_ref,
    kv_hbm,
    query_hbm,
    hidden_hbm,
    proj_hbm,
    slot_hbm,
    send_ref,
    max_ref,
    acc_ref,
    line_buf,
    kv_buf,
    query_ref,
    hidden_ref,
    proj_buf,
    slot_ref,
    line_sem,
    kv_sem,
    other_sem,
    *,
    segments,
    rows,
    pitch,
    top,
    together,
):
    def kv_copy(b):
        at = pl.ds(0, rows)
        return pltpu.make_async_copy(kv_hbm.at[b, at], kv_buf.at[b], kv_sem.at[b])

    def line_copy(b):
        at = pl.ds(rows, pitch - rows)
        return pltpu.make_async_copy(kv_hbm.at[b, at], line_buf.at[b], line_sem.at[b])

    query_copy, hidden_copy, proj_copy, slot_copy = [
        pltpu.make_async_copy(src, dst, other_sem.at[i])
        for i, (src, dst) in enumerate(
            (
                (query_hbm, query_ref),
                (hidden_hbm, hidden_ref),
                (proj_hbm, proj_buf),
                (slot_hbm, slot_ref),
            )
        )
    ]
    for b in range(segments):
        line_copy(b).start()
    query_copy.start()
    for b in range(segments):
        kv_copy(b).start()
    proj_copy.start()
    hidden_copy.start()
    slot_copy.start()
    tokens = query_ref.shape[0]
    heads = query_ref.shape[1] // LANES
    scale = LANES**-0.5 * 1.4426950408889634
    max_ref[...] = jnp.full(max_ref.shape, NEG, F32)
    acc_ref[...] = jnp.zeros(acc_ref.shape, F32)
    extra = acc_ref.shape[1] - LANES
    for b in range(segments):
        line_copy(b).wait()
    seq, exp = place_ref[0], place_ref[1]
    total = jnp.zeros((16, LANES), F32)
    lane = iota((16, LANES), 1)
    for s in range(segments):
        line = line_buf[s, :, 0:LANES].astype(F32)
        take = jnp.logical_or(seq > s, jnp.logical_and(seq == s, lane < exp))
        total = total + jnp.where(take, line, 0.0)
    offset = (jnp.sum(total) * (1.0 / 16.0)).astype(jnp.int32)
    ends = []
    for g in range(lens_ref.shape[0]):
        offset = offset + lens_ref[g]
        ends.append(offset)
    size = together * tokens
    group = (iota((1, size), 1) % tokens) // GROUP
    limits = jnp.zeros((1, size), jnp.int32)
    for g, end in enumerate(ends):
        limits = jnp.where(group == g, end, limits)
    ones = jnp.ones((extra, rows), BF16)

    def block(masked):
        def body(step, carry):
            keys, talls = [], []
            for i in range(SUB):
                b = step * SUB + i
                kv_copy(b).wait()
                keys.append(kv_buf[b, :, 0:LANES])
                values = jnp.concatenate(
                    [kv_buf[b, r : r + LANES, LANES : 2 * LANES] for r in range(0, rows, LANES)],
                    axis=1,
                )
                talls.append(jnp.concatenate([values, ones], axis=0))
            for g in range(heads // together):
                q = jnp.concatenate(
                    [
                        query_ref[:, i * LANES : (i + 1) * LANES]
                        for i in range(g * together, (g + 1) * together)
                    ],
                    axis=0,
                )
                old = max_ref[g]
                new, scores = old, []
                for i in range(SUB):
                    s = dot(keys[i], q, ((1,), (1,)))
                    if masked:
                        place = iota((rows, size), 0) + (step * SUB + i) * rows
                        s = jnp.where(place < limits, s, NEG)
                    new = jnp.maximum(new, jnp.max(s, axis=0, keepdims=True))
                    scores.append(s)
                max_ref[g] = new
                acc = acc_ref[g] * jnp.exp2((old - new) * scale)
                for i in range(SUB):
                    w = jnp.exp2((scores[i] - new) * scale).astype(BF16)
                    acc = acc + dot(talls[i], w)
                acc_ref[g] = acc
            return carry

        return body

    full = ends[0] // (rows * SUB)
    last = (ends[-1] + rows * SUB - 1) // (rows * SUB)
    query_copy.wait()
    lax.fori_loop(0, full, block(False), 0)
    lax.fori_loop(full, last, block(True), 0)

    def unused(b, carry):
        kv_copy(b).wait()
        return carry

    lax.fori_loop(last * SUB, segments, unused, 0)
    attended = []
    for g in range(heads // together):
        acc = acc_ref[g]
        part = (acc[:LANES, :] / acc[LANES : LANES + 1, :]).astype(BF16)
        attended += [part[:, i * tokens : (i + 1) * tokens] for i in range(together)]
    proj_copy.wait()
    hidden_copy.wait()
    slot_copy.wait()
    mixed = hidden_ref[...].astype(F32) + dot(
        jnp.concatenate(attended, axis=0), proj_buf[...], ((0,), (0,))
    )
    chunks = hidden_ref.shape[1] // LANES
    slots = send_ref.shape[0] // chunks
    wide = dot(placed(slot_ref[...], top, slots), mixed.astype(BF16)).astype(BF16)

    def store(first, part):
        send_ref[first : first + part.shape[0], :] = part

    fold_rows(wide, fold_matrix(BLOCK, chunks), store)


def prepare_kernel(cot_ref, weight_ref, back_ref, c_ref, down_buf, down_sem):
    slots, width = c_ref.shape
    chunks = width // LANES
    shards, _, ff = down_buf.shape
    copies = [
        pltpu.make_async_copy(
            weight_ref.at[s, pl.ds(2 * LANES, LANES)], down_buf.at[s], down_sem.at[s]
        )
        for s in range(shards)
    ]
    for copy in copies:
        copy.start()
    unfold_rows(
        lambda f, n: cot_ref[f : f + n, :], slots, chunks, unfold_matrix(BLOCK, chunks), c_ref
    )
    c = c_ref[...]
    for copy in copies:
        copy.wait()
    step = 256
    for j in range(0, ff, step):
        w_down = jnp.concatenate(
            [
                jnp.concatenate(
                    [down_buf[s, :, i : i + LANES] for i in range(j, j + step, LANES)], axis=0
                )
                for s in range(shards)
            ],
            axis=1,
        )
        back_ref[:, j : j + step] = dot(c, w_down, ((1,), (1,)))


def expert_kernel(
    row_ref,
    weight_ref,
    back_ref,
    out_ref,
    x_ref,
    both_ref,
    gate_buf,
    up_buf,
    back_buf,
    weight_sem,
    back_sem,
    *,
    capacity,
):
    slots, width = x_ref.shape
    chunks = width // LANES
    shards = weight_ref.shape[0]
    rows = gate_buf.shape[0] // shards
    ff = weight_ref.shape[2]
    gate_copies, up_copies = [
        [
            pltpu.make_async_copy(
                weight_ref.at[s, pl.ds(i * rows, rows)],
                buf.at[pl.ds(s * rows, rows)],
                weight_sem.at[s, i],
            )
            for s in range(shards)
        ]
        for i, buf in enumerate((gate_buf, up_buf))
    ]
    back_copy = pltpu.make_async_copy(back_ref, back_buf, back_sem)
    for copy in gate_copies + up_copies + [back_copy]:
        copy.start()
    unfold_rows(
        lambda f, n: row_ref[f : f + n, :], slots, chunks, unfold_matrix(BLOCK, chunks), x_ref
    )
    x = x_ref[...]
    step = 256
    gate_sum = jnp.zeros((slots, 1), F32)
    for j in range(ff // step):
        at = slice(j * step, (j + 1) * step)
        if j == 0:
            for copy in gate_copies:
                copy.wait()
        gate_lin = dot(x, gate_buf[:, at])
        if j == 0:
            for copy in up_copies:
                copy.wait()
        up_lin = dot(x, up_buf[:, at])
        if j == 0:
            back_copy.wait()
        back = back_buf[:, at]
        sig = 0.5 * jnp.tanh(0.5 * gate_lin) + 0.5
        swish = gate_lin * sig
        up_back = back * swish
        gate_sum = gate_sum + jnp.sum(up_back * up_lin, axis=1, keepdims=True)
        gate_back = back * up_lin * (sig + swish * (1.0 - sig))
        both_ref[:, at] = gate_back.astype(BF16)
        both_ref[:, ff + j * step : ff + (j + 1) * step] = up_back.astype(BF16)
    both = both_ref[...]
    for n in range(0, width, step):
        w = jnp.concatenate([gate_buf[n : n + step, :], up_buf[n : n + step, :]], axis=1)
        x_ref[:, n : n + step] = dot(both, w, ((1,), (1,))).astype(BF16)
    experts = slots // capacity
    each = capacity * chunks

    def store(first, rows):
        size = rows.shape[0]
        at = first
        while at < first + size:
            e, r = at // each, at % each
            n = min(each - r, first + size - at)
            out_ref[e, r : r + n, :] = rows[at - first : at - first + n, :]
            at += n

    fold_rows(x_ref[...], fold_matrix(BLOCK, chunks), store)
    high = gate_sum.astype(BF16)
    low = (gate_sum - high.astype(F32)).astype(BF16)
    slot, lane = iota((slots, LANES), 0), iota((slots, LANES), 1)
    rank = slot % capacity
    spread = jnp.where(rank == lane, high.astype(F32), 0.0) + jnp.where(
        rank + 16 == lane, low.astype(F32), 0.0
    )
    owner = as_bf16(iota((experts, slots), 0) == iota((experts, slots), 1) // capacity)
    lines = dot(owner, spread.astype(BF16)).astype(BF16)
    for e in range(experts):
        out_ref[e, each:, :] = jnp.broadcast_to(
            lines[e : e + 1, :], (out_ref.shape[1] - each, LANES)
        )


def combine_kernel(
    back_ref, line_ref, ids_ref, gate_ref, slot_ref, grad_ref, gates_ref, wide_ref, *, capacity
):
    top, tokens = ids_ref.shape
    slots, width = wide_ref.shape
    chunks = width // LANES
    experts = slots // capacity
    each = capacity * chunks

    def load(first, count):
        parts, at = [], first
        while at < first + count:
            e, r = at // each, at % each
            n = min(each - r, first + count - at)
            parts.append(back_ref[e, r : r + n, :])
            at += n
        return jnp.concatenate(parts, axis=0)

    unfold_rows(load, slots, chunks, unfold_matrix(BLOCK, chunks), wide_ref)
    both = slot_ref[...]
    spread = placed(both, top, slots)
    grad_ref[...] = dot(spread, wide_ref[...], ((0,), (0,)))
    lines = line_ref[...]
    expert = iota((experts, tokens), 0)
    rank = iota((LANES, tokens), 0)
    out = []
    for k in range(top):
        own = as_bf16(expert == ids_ref[k : k + 1, :])
        found = dot(lines, own, ((0,), (0,)))
        mine = both[top + k : top + k + 1, :]
        take = jnp.logical_or(rank == mine, rank == mine + 16)
        value = jnp.sum(jnp.where(take, found, 0.0), axis=0, keepdims=True)
        out.append(value / gate_ref[k : k + 1, :].astype(F32))
    gates_ref[...] = jnp.concatenate(out, axis=0).astype(BF16)


HBM = pl.BlockSpec(memory_space=pltpu.HBM)
TOGETHER = 8
SUB = 4


def attend(place, lens, kv, queries, hidden, proj, slot_table, *, rows, slots):
    tokens, width = hidden.shape
    segments, pitch = kv.shape[0], kv.shape[1]
    top = slot_table.shape[0] // 2
    heads, chunks = queries.shape[1] // LANES, width // LANES
    return pl.pallas_call(
        functools.partial(
            attend_kernel, segments=segments, rows=rows, pitch=pitch, top=top, together=TOGETHER
        ),
        out_shape=jax.ShapeDtypeStruct((slots * chunks, LANES), BF16),
        in_specs=[SMEM, SMEM] + [HBM] * 5,
        out_specs=vmem(1)[0],
        scratch_shapes=[
            pltpu.VMEM((heads // TOGETHER, 1, TOGETHER * tokens), F32),
            pltpu.VMEM((heads // TOGETHER, LANES + 16, TOGETHER * tokens), F32),
            pltpu.VMEM((segments, pitch - rows, 2 * LANES), BF16),
            pltpu.VMEM((segments, rows, 2 * LANES), BF16),
            pltpu.VMEM(queries.shape, BF16),
            pltpu.VMEM(hidden.shape, BF16),
            pltpu.VMEM(proj.shape, BF16),
            pltpu.VMEM(slot_table.shape, jnp.int32),
            pltpu.SemaphoreType.DMA((segments,)),
            pltpu.SemaphoreType.DMA((segments,)),
            pltpu.SemaphoreType.DMA((4,)),
        ],
        compiler_params=params(58),
        cost_estimate=pl.CostEstimate(flops=0, bytes_accessed=0, transcendentals=0),
        name="attend",
    )(place, lens, kv, queries, hidden, proj, slot_table)


def expert(rows, weights, back, *, capacity):
    slots, (shards, _, ff) = back.shape[0], weights.shape
    width = shards * LANES
    chunks = width // LANES
    return pl.pallas_call(
        functools.partial(expert_kernel, capacity=capacity),
        out_shape=jax.ShapeDtypeStruct((slots // capacity, capacity * chunks + 8, LANES), BF16),
        in_specs=vmem(1) + [HBM] * 2,
        out_specs=vmem(1)[0],
        scratch_shapes=[
            pltpu.VMEM((slots, width), BF16),
            pltpu.VMEM((slots, 2 * ff), BF16),
            pltpu.VMEM((width, ff), BF16),
            pltpu.VMEM((width, ff), BF16),
            pltpu.VMEM(back.shape, F32),
            pltpu.SemaphoreType.DMA((shards, 2)),
            pltpu.SemaphoreType.DMA(()),
        ],
        compiler_params=params(50),
        name="expert",
    )(rows, weights, back)


def exchange(rows):
    return lax.all_to_all(rows, "exp", split_axis=0, concat_axis=0, tiled=True)


def local(
    hidden,
    queries,
    thinker_keys,
    thinker_values,
    thinker_lengths,
    out_proj,
    expert_ids,
    gate_values,
    w_gate,
    w_up,
    w_down,
    cotangent,
):
    tokens, width = hidden.shape
    top = expert_ids.shape[1]
    experts, shards = lax.axis_size("exp"), lax.axis_size("seq")
    capacity = tokens * top * 5 // (4 * experts)
    slots = experts * capacity
    chunks = width // LANES
    each = capacity * chunks
    ff = w_gate.shape[2]
    own_rows = thinker_keys.shape[0]
    rows = experts * own_rows
    pitch = rows + 16
    place = jnp.stack([lax.axis_index("seq"), lax.axis_index("exp")]).astype(jnp.int32)
    ids, gates = expert_ids.T, gate_values.T

    packed = pl.pallas_call(
        pack_kernel,
        out_shape=jax.ShapeDtypeStruct((experts, own_rows, 3 * LANES), BF16),
        in_specs=[SMEM, HBM, HBM],
        out_specs=vmem(1)[0],
        scratch_shapes=[
            pltpu.VMEM(thinker_keys.shape, BF16),
            pltpu.VMEM(thinker_values.shape, BF16),
            pltpu.SemaphoreType.DMA((2,)),
        ],
        compiler_params=params(58),
        name="pack",
    )(thinker_lengths, thinker_keys, thinker_values)
    kv_rows = exchange(packed)

    slot_table, send_cot = pl.pallas_call(
        functools.partial(dispatch_kernel, experts=experts, capacity=capacity),
        out_shape=(
            jax.ShapeDtypeStruct((2 * top, tokens), jnp.int32),
            jax.ShapeDtypeStruct((slots * chunks, LANES), BF16),
        ),
        in_specs=vmem(3),
        out_specs=tuple(vmem(2)),
        compiler_params=params(24),
        name="dispatch",
    )(ids, gates, cotangent)

    segment = pl.pallas_call(
        functools.partial(segment_kernel, rows=own_rows),
        out_shape=jax.ShapeDtypeStruct((pitch, 2 * LANES), BF16),
        in_specs=vmem(1),
        out_specs=vmem(1)[0],
        compiler_params=params(16),
        name="segment",
    )(kv_rows.reshape(rows, 3 * LANES))
    lower = jnp.concatenate(
        [w_down[0][i * LANES : (i + 1) * LANES, :] for i in range(ff // LANES)], axis=1
    )
    shard = jnp.concatenate([w_gate[0], w_up[0], lower], axis=0)
    segment, send_cot, shard = lax.optimization_barrier((segment, send_cot, shard))
    kv_all = lax.all_gather(segment, "seq", axis=0, tiled=True)
    recv_cot = exchange(send_cot.reshape(experts, each, LANES))
    weights = lax.all_gather(shard, "seq", axis=0, tiled=False)

    send_rows = attend(
        place,
        thinker_lengths,
        kv_all.reshape(shards, pitch, 2 * LANES),
        queries,
        hidden,
        out_proj,
        slot_table,
        rows=rows,
        slots=slots,
    )
    send_rows, recv_cot = lax.optimization_barrier((send_rows, recv_cot))
    recv_rows = exchange(send_rows.reshape(experts, each, LANES))
    down_back = pl.pallas_call(
        prepare_kernel,
        out_shape=jax.ShapeDtypeStruct((slots, ff), F32),
        in_specs=[vmem(1)[0], HBM],
        out_specs=vmem(1)[0],
        scratch_shapes=[
            pltpu.VMEM((slots, width), BF16),
            pltpu.VMEM((shards, LANES, ff), BF16),
            pltpu.SemaphoreType.DMA((shards,)),
        ],
        compiler_params=params(50),
        cost_estimate=pl.CostEstimate(
            flops=40 * slots * width * ff, bytes_accessed=0, transcendentals=0
        ),
        name="prepare",
    )(recv_cot.reshape(slots * chunks, LANES), weights)
    back = expert(
        recv_rows.reshape(slots * chunks, LANES), weights, down_back, capacity=capacity
    )
    home = exchange(back)

    grad_input, grad_gates = pl.pallas_call(
        functools.partial(combine_kernel, capacity=capacity),
        out_shape=(
            jax.ShapeDtypeStruct((tokens, width), F32),
            jax.ShapeDtypeStruct((top, tokens), BF16),
        ),
        in_specs=vmem(5),
        out_specs=tuple(vmem(2)),
        scratch_shapes=[pltpu.VMEM((slots, width), BF16)],
        compiler_params=params(24),
        name="combine",
    )(home, home[:, each, :], ids, gates, slot_table)
    return grad_input, grad_gates.T


def solution(mesh):
    both = P(("seq", "exp"), None)
    return jax.shard_map(
        local,
        mesh=mesh,
        in_specs=(
            both,
            both,
            both,
            both,
            P(("seq", "exp")),
            P(),
            both,
            both,
            P("exp", "seq", None),
            P("exp", "seq", None),
            P("exp", None, "seq"),
            both,
        ),
        out_specs=(both, both),
        check_vma=False,
    )
```

```python
import functools

import jax
import jax.numpy as jnp
from jax import lax
from jax.experimental import pallas as pl
from jax.experimental.pallas import tpu as pltpu
from jax.sharding import PartitionSpec as P

GROUP = 32
NEG = -1e30
LANES = 128
F32 = jnp.float32
BF16 = jnp.bfloat16
MIB = 1 << 20


def params(mib):
    return pltpu.CompilerParams(vmem_limit_bytes=mib * MIB)


def vmem(count):
    return [pl.BlockSpec(memory_space=pltpu.VMEM)] * count


SMEM = pl.BlockSpec(memory_space=pltpu.SMEM)


def iota(shape, dim):
    return lax.broadcasted_iota(jnp.int32, shape, dim)


def dot(a, b, dims=((1,), (0,))):
    return lax.dot_general(a, b, (dims, ((), ())), preferred_element_type=F32)


def as_bf16(mask):
    return jnp.where(mask, 1.0, 0.0).astype(BF16)


def fold_matrix(slots, chunks):
    rows = slots * chunks
    row, col = iota((rows, rows), 0), iota((rows, rows), 1)
    return as_bf16((row // chunks) + (row % chunks) * slots == col)


def unfold_matrix(slots, chunks):
    rows = slots * chunks
    row, col = iota((rows, rows), 0), iota((rows, rows), 1)
    return as_bf16((col // chunks) + (col % chunks) * slots == row)


BLOCK = 32


def fold_rows(wide, matrix, store):
    chunks = wide.shape[1] // LANES
    size = BLOCK * chunks

    def stacked(b):
        part = wide[b * BLOCK : (b + 1) * BLOCK, :]
        return jnp.concatenate(
            [part[:, c * LANES : (c + 1) * LANES] for c in range(chunks)], axis=0
        )

    for b in range(0, wide.shape[0] // BLOCK, 2):
        two = jnp.concatenate([stacked(b), stacked(b + 1)], axis=1)
        out = dot(matrix, two).astype(BF16)
        store(b * size, out[:, :LANES])
        store((b + 1) * size, out[:, LANES:])


def unfold_rows(load, slots, chunks, matrix, ref):
    size = BLOCK * chunks
    for b in range(0, slots // BLOCK, 2):
        two = jnp.concatenate([load(b * size, size), load((b + 1) * size, size)], axis=1)
        out = dot(matrix, two).astype(BF16)
        for half in range(2):
            for c in range(chunks):
                ref[
                    (b + half) * BLOCK : (b + half + 1) * BLOCK, c * LANES : (c + 1) * LANES
                ] = out[c * BLOCK : (c + 1) * BLOCK, half * LANES : (half + 1) * LANES]


def pack_kernel(lens_ref, key_hbm, value_hbm, out_ref, key_ref, value_ref, sem):
    copies = [
        pltpu.make_async_copy(key_hbm, key_ref, sem.at[0]),
        pltpu.make_async_copy(value_hbm, value_ref, sem.at[1]),
    ]
    for copy in copies:
        copy.start()
    copies_out = out_ref.shape[0]
    total = lens_ref[0]
    for i in range(1, lens_ref.shape[0]):
        total = total + lens_ref[i]
    half = key_ref.shape[0] // 2
    tot = jnp.full((half, LANES), total.astype(F32), F32)
    for copy in copies:
        copy.wait()
    key, value = key_ref[...].astype(F32), value_ref[...].astype(F32)
    tiles = (key[:half], key[half:], value[:half], value[half:], tot)
    for i, tile in enumerate(tiles):
        out_ref[:, i] = jnp.broadcast_to(tile[None], (copies_out,) + tile.shape).astype(BF16)


def segment_kernel(in_ref, out_ref):
    sources, _, half, _ = in_ref.shape
    count = sources * 2 * half

    def whole(i):
        parts = [in_ref[:, i].astype(F32), in_ref[:, i + 1].astype(F32)]
        return jnp.concatenate(parts, axis=1).reshape(count, LANES)

    keys, values = whole(0), whole(2)
    out_ref[0:count, 0:LANES] = keys.astype(BF16)
    for i in range(0, count, LANES):
        out_ref[i : i + LANES, LANES : 2 * LANES] = values[i : i + LANES, :].T.astype(BF16)
    tot = in_ref[:, 4].astype(F32)
    source, row, lane = iota(tot.shape, 0), iota(tot.shape, 1), iota(tot.shape, 2)
    take = jnp.logical_and(row == 0, source == lane)
    line = jnp.sum(jnp.sum(jnp.where(take, tot, 0.0), axis=0), axis=0, keepdims=True)
    more = out_ref.shape[0] - count
    line = jnp.broadcast_to(line, (more, LANES))
    out_ref[count:, :] = jnp.concatenate([line, jnp.zeros_like(line)], axis=1).astype(BF16)


def placed(slot_rows, top, slots, values=None):
    tokens = slot_rows.shape[1]
    place = iota((slots, tokens), 0)
    out = jnp.zeros((slots, tokens), F32)
    for k in range(top):
        value = 1.0 if values is None else values[k : k + 1, :]
        out = jnp.where(place == slot_rows[k : k + 1, :], value, out)
    return out.astype(BF16)


def dispatch_kernel(ids_ref, gate_ref, cot_ref, slot_ref, send_ref, *, experts, capacity):
    top, tokens = ids_ref.shape
    ids = ids_ref[...]
    expert = iota((experts, tokens), 0)
    named = jnp.zeros((experts, tokens), F32)
    for k in range(top):
        named = jnp.where(expert == ids[k : k + 1, :], 1.0, named)
    earlier = as_bf16(iota((tokens, tokens), 0) < iota((tokens, tokens), 1))
    before = dot(named.astype(BF16), earlier)
    slot_rows, ranks = [], []
    for k in range(top):
        own = ids[k : k + 1, :]
        rank = jnp.sum(jnp.where(expert == own, before, 0.0), axis=0, keepdims=True)
        rank = rank.astype(jnp.int32)
        ranks.append(rank)
        slot_rows.append(own * capacity + rank)
    both = jnp.concatenate(slot_rows + ranks, axis=0)
    slot_ref[...] = both
    slots = experts * capacity
    spread = placed(both, top, slots, gate_ref[...].astype(F32))
    wide = dot(spread, cot_ref[...]).astype(BF16)
    chunks = cot_ref.shape[1] // LANES

    def store(first, rows):
        send_ref[first : first + rows.shape[0], :] = rows

    fold_rows(wide, fold_matrix(BLOCK, chunks), store)


def attend_kernel(
    place_ref,
    lens_ref,
    kv_hbm,
    query_hbm,
    hidden_hbm,
    proj_hbm,
    slot_hbm,
    send_ref,
    max_ref,
    acc_ref,
    line_buf,
    kv_buf,
    query_ref,
    hidden_ref,
    proj_buf,
    slot_ref,
    line_sem,
    kv_sem,
    other_sem,
    *,
    segments,
    rows,
    pitch,
    top,
    together,
):
    def kv_copy(b):
        at = pl.ds(0, rows)
        return pltpu.make_async_copy(kv_hbm.at[b, at], kv_buf.at[b], kv_sem.at[b])

    def line_copy(b):
        at = pl.ds(rows, pitch - rows)
        return pltpu.make_async_copy(kv_hbm.at[b, at], line_buf.at[b], line_sem.at[b])

    query_copy, hidden_copy, proj_copy, slot_copy = [
        pltpu.make_async_copy(src, dst, other_sem.at[i])
        for i, (src, dst) in enumerate(
            (
                (query_hbm, query_ref),
                (hidden_hbm, hidden_ref),
                (proj_hbm, proj_buf),
                (slot_hbm, slot_ref),
            )
        )
    ]
    for b in range(segments):
        line_copy(b).start()
    query_copy.start()
    for b in range(segments):
        kv_copy(b).start()
    proj_copy.start()
    hidden_copy.start()
    slot_copy.start()
    tokens = query_ref.shape[0]
    heads = query_ref.shape[1] // LANES
    scale = LANES**-0.5 * 1.4426950408889634
    max_ref[...] = jnp.full(max_ref.shape, NEG, F32)
    acc_ref[...] = jnp.zeros(acc_ref.shape, F32)
    extra = acc_ref.shape[1] - LANES
    for b in range(segments):
        line_copy(b).wait()
    seq, exp = place_ref[0], place_ref[1]
    total = jnp.zeros((16, LANES), F32)
    lane = iota((16, LANES), 1)
    for s in range(segments):
        line = line_buf[s, :, 0:LANES].astype(F32)
        take = jnp.logical_or(seq > s, jnp.logical_and(seq == s, lane < exp))
        total = total + jnp.where(take, line, 0.0)
    offset = (jnp.sum(total) * (1.0 / 16.0)).astype(jnp.int32)
    ends = []
    for g in range(lens_ref.shape[0]):
        offset = offset + lens_ref[g]
        ends.append(offset)
    size = together * tokens
    group = (iota((1, size), 1) % tokens) // GROUP
    limits = jnp.zeros((1, size), jnp.int32)
    for g, end in enumerate(ends):
        limits = jnp.where(group == g, end, limits)
    ones = jnp.ones((extra, rows), BF16)

    def block(masked):
        def body(step, carry):
            keys, talls = [], []
            for i in range(SUB):
                b = step * SUB + i
                kv_copy(b).wait()
                keys.append(kv_buf[b, :, 0:LANES])
                values = jnp.concatenate(
                    [kv_buf[b, r : r + LANES, LANES : 2 * LANES] for r in range(0, rows, LANES)],
                    axis=1,
                )
                talls.append(jnp.concatenate([values, ones], axis=0))
            for g in range(heads // together):
                q = jnp.concatenate(
                    [
                        query_ref[:, i * LANES : (i + 1) * LANES]
                        for i in range(g * together, (g + 1) * together)
                    ],
                    axis=0,
                )
                old = max_ref[g]
                new, scores = old, []
                for i in range(SUB):
                    s = dot(keys[i], q, ((1,), (1,)))
                    if masked:
                        place = iota((rows, size), 0) + (step * SUB + i) * rows
                        s = jnp.where(place < limits, s, NEG)
                    new = jnp.maximum(new, jnp.max(s, axis=0, keepdims=True))
                    scores.append(s)
                max_ref[g] = new
                acc = acc_ref[g] * jnp.exp2((old - new) * scale)
                for i in range(SUB):
                    w = jnp.exp2((scores[i] - new) * scale).astype(BF16)
                    acc = acc + dot(talls[i], w)
                acc_ref[g] = acc
            return carry

        return body

    full = ends[0] // (rows * SUB)
    last = (ends[-1] + rows * SUB - 1) // (rows * SUB)
    query_copy.wait()
    lax.fori_loop(0, full, block(False), 0)
    lax.fori_loop(full, last, block(True), 0)

    def unused(b, carry):
        kv_copy(b).wait()
        return carry

    lax.fori_loop(last * SUB, segments, unused, 0)
    attended = []
    for g in range(heads // together):
        acc = acc_ref[g]
        part = (acc[:LANES, :] / acc[LANES : LANES + 1, :]).astype(BF16)
        attended += [part[:, i * tokens : (i + 1) * tokens] for i in range(together)]
    proj_copy.wait()
    hidden_copy.wait()
    slot_copy.wait()
    mixed = hidden_ref[...].astype(F32) + dot(
        jnp.concatenate(attended, axis=0), proj_buf[...], ((0,), (0,))
    )
    chunks = hidden_ref.shape[1] // LANES
    slots = send_ref.shape[0] // chunks
    wide = dot(placed(slot_ref[...], top, slots), mixed.astype(BF16)).astype(BF16)

    def store(first, part):
        send_ref[first : first + part.shape[0], :] = part

    fold_rows(wide, fold_matrix(BLOCK, chunks), store)


def prepare_kernel(cot_ref, weight_ref, back_ref, c_ref, down_buf, down_sem):
    slots, width = c_ref.shape
    chunks = width // LANES
    shards, _, ff = down_buf.shape
    copies = [
        pltpu.make_async_copy(
            weight_ref.at[s, pl.ds(2 * LANES, LANES)], down_buf.at[s], down_sem.at[s]
        )
        for s in range(shards)
    ]
    for copy in copies:
        copy.start()
    unfold_rows(
        lambda f, n: cot_ref[f : f + n, :], slots, chunks, unfold_matrix(BLOCK, chunks), c_ref
    )
    c = c_ref[...]
    for copy in copies:
        copy.wait()
    step = 256
    for j in range(0, ff, step):
        w_down = jnp.concatenate(
            [
                jnp.concatenate(
                    [down_buf[s, :, i : i + LANES] for i in range(j, j + step, LANES)], axis=0
                )
                for s in range(shards)
            ],
            axis=1,
        )
        back_ref[:, j : j + step] = dot(c, w_down, ((1,), (1,)))


def expert_kernel(
    row_ref,
    weight_ref,
    back_ref,
    out_ref,
    x_ref,
    both_ref,
    gate_buf,
    up_buf,
    back_buf,
    weight_sem,
    back_sem,
    *,
    capacity,
):
    slots, width = x_ref.shape
    chunks = width // LANES
    shards = weight_ref.shape[0]
    rows = gate_buf.shape[0] // shards
    ff = weight_ref.shape[2]
    gate_copies, up_copies = [
        [
            pltpu.make_async_copy(
                weight_ref.at[s, pl.ds(i * rows, rows)],
                buf.at[pl.ds(s * rows, rows)],
                weight_sem.at[s, i],
            )
            for s in range(shards)
        ]
        for i, buf in enumerate((gate_buf, up_buf))
    ]
    back_copy = pltpu.make_async_copy(back_ref, back_buf, back_sem)
    for copy in gate_copies + up_copies + [back_copy]:
        copy.start()
    unfold_rows(
        lambda f, n: row_ref[f : f + n, :], slots, chunks, unfold_matrix(BLOCK, chunks), x_ref
    )
    x = x_ref[...]
    step = 256
    gate_sum = jnp.zeros((slots, 1), F32)
    for j in range(ff // step):
        at = slice(j * step, (j + 1) * step)
        if j == 0:
            for copy in gate_copies:
                copy.wait()
        gate_lin = dot(x, gate_buf[:, at])
        if j == 0:
            for copy in up_copies:
                copy.wait()
        up_lin = dot(x, up_buf[:, at])
        if j == 0:
            back_copy.wait()
        back = back_buf[:, at]
        sig = 0.5 * jnp.tanh(0.5 * gate_lin) + 0.5
        swish = gate_lin * sig
        up_back = back * swish
        gate_sum = gate_sum + jnp.sum(up_back * up_lin, axis=1, keepdims=True)
        gate_back = back * up_lin * (sig + swish * (1.0 - sig))
        both_ref[:, at] = gate_back.astype(BF16)
        both_ref[:, ff + j * step : ff + (j + 1) * step] = up_back.astype(BF16)
    both = both_ref[...]
    for n in range(0, width, step):
        w = jnp.concatenate([gate_buf[n : n + step, :], up_buf[n : n + step, :]], axis=1)
        x_ref[:, n : n + step] = dot(both, w, ((1,), (1,))).astype(BF16)
    experts = slots // capacity
    each = capacity * chunks

    def store(first, rows):
        size = rows.shape[0]
        at = first
        while at < first + size:
            e, r = at // each, at % each
            n = min(each - r, first + size - at)
            out_ref[e, r : r + n, :] = rows[at - first : at - first + n, :]
            at += n

    fold_rows(x_ref[...], fold_matrix(BLOCK, chunks), store)
    high = gate_sum.astype(BF16)
    low = (gate_sum - high.astype(F32)).astype(BF16)
    slot, lane = iota((slots, LANES), 0), iota((slots, LANES), 1)
    rank = slot % capacity
    spread = jnp.where(rank == lane, high.astype(F32), 0.0) + jnp.where(
        rank + 16 == lane, low.astype(F32), 0.0
    )
    owner = as_bf16(iota((experts, slots), 0) == iota((experts, slots), 1) // capacity)
    lines = dot(owner, spread.astype(BF16)).astype(BF16)
    for e in range(experts):
        out_ref[e, each:, :] = jnp.broadcast_to(
            lines[e : e + 1, :], (out_ref.shape[1] - each, LANES)
        )


def combine_kernel(
    back_ref, line_ref, ids_ref, gate_ref, slot_ref, grad_ref, gates_ref, wide_ref, *, capacity
):
    top, tokens = ids_ref.shape
    slots, width = wide_ref.shape
    chunks = width // LANES
    experts = slots // capacity
    each = capacity * chunks

    def load(first, count):
        parts, at = [], first
        while at < first + count:
            e, r = at // each, at % each
            n = min(each - r, first + count - at)
            parts.append(back_ref[e, r : r + n, :])
            at += n
        return jnp.concatenate(parts, axis=0)

    unfold_rows(load, slots, chunks, unfold_matrix(BLOCK, chunks), wide_ref)
    both = slot_ref[...]
    spread = placed(both, top, slots)
    grad_ref[...] = dot(spread, wide_ref[...], ((0,), (0,)))
    lines = line_ref[...]
    expert = iota((experts, tokens), 0)
    rank = iota((LANES, tokens), 0)
    out = []
    for k in range(top):
        own = as_bf16(expert == ids_ref[k : k + 1, :])
        found = dot(lines, own, ((0,), (0,)))
        mine = both[top + k : top + k + 1, :]
        take = jnp.logical_or(rank == mine, rank == mine + 16)
        value = jnp.sum(jnp.where(take, found, 0.0), axis=0, keepdims=True)
        out.append(value / gate_ref[k : k + 1, :].astype(F32))
    gates_ref[...] = jnp.concatenate(out, axis=0).astype(BF16)


HBM = pl.BlockSpec(memory_space=pltpu.HBM)
TOGETHER = 8
SUB = 4


def attend(place, lens, kv, queries, hidden, proj, slot_table, *, rows, slots):
    tokens, width = hidden.shape
    segments, pitch = kv.shape[0], kv.shape[1]
    top = slot_table.shape[0] // 2
    heads, chunks = queries.shape[1] // LANES, width // LANES
    return pl.pallas_call(
        functools.partial(
            attend_kernel, segments=segments, rows=rows, pitch=pitch, top=top, together=TOGETHER
        ),
        out_shape=jax.ShapeDtypeStruct((slots * chunks, LANES), BF16),
        in_specs=[SMEM, SMEM] + [HBM] * 5,
        out_specs=vmem(1)[0],
        scratch_shapes=[
            pltpu.VMEM((heads // TOGETHER, 1, TOGETHER * tokens), F32),
            pltpu.VMEM((heads // TOGETHER, LANES + 16, TOGETHER * tokens), F32),
            pltpu.VMEM((segments, pitch - rows, 2 * LANES), BF16),
            pltpu.VMEM((segments, rows, 2 * LANES), BF16),
            pltpu.VMEM(queries.shape, BF16),
            pltpu.VMEM(hidden.shape, BF16),
            pltpu.VMEM(proj.shape, BF16),
            pltpu.VMEM(slot_table.shape, jnp.int32),
            pltpu.SemaphoreType.DMA((segments,)),
            pltpu.SemaphoreType.DMA((segments,)),
            pltpu.SemaphoreType.DMA((4,)),
        ],
        compiler_params=params(58),
        cost_estimate=pl.CostEstimate(flops=0, bytes_accessed=0, transcendentals=0),
        name="attend",
    )(place, lens, kv, queries, hidden, proj, slot_table)


def expert(rows, weights, back, *, capacity):
    slots, (shards, _, ff) = back.shape[0], weights.shape
    width = shards * LANES
    chunks = width // LANES
    return pl.pallas_call(
        functools.partial(expert_kernel, capacity=capacity),
        out_shape=jax.ShapeDtypeStruct((slots // capacity, capacity * chunks + 8, LANES), BF16),
        in_specs=vmem(1) + [HBM] * 2,
        out_specs=vmem(1)[0],
        scratch_shapes=[
            pltpu.VMEM((slots, width), BF16),
            pltpu.VMEM((slots, 2 * ff), BF16),
            pltpu.VMEM((width, ff), BF16),
            pltpu.VMEM((width, ff), BF16),
            pltpu.VMEM(back.shape, F32),
            pltpu.SemaphoreType.DMA((shards, 2)),
            pltpu.SemaphoreType.DMA(()),
        ],
        compiler_params=params(50),
        name="expert",
    )(rows, weights, back)


def exchange(rows):
    return lax.all_to_all(rows, "exp", split_axis=0, concat_axis=0, tiled=True)


def local(
    hidden,
    queries,
    thinker_keys,
    thinker_values,
    thinker_lengths,
    out_proj,
    expert_ids,
    gate_values,
    w_gate,
    w_up,
    w_down,
    cotangent,
):
    tokens, width = hidden.shape
    top = expert_ids.shape[1]
    experts, shards = lax.axis_size("exp"), lax.axis_size("seq")
    capacity = tokens * top * 5 // (4 * experts)
    slots = experts * capacity
    chunks = width // LANES
    each = capacity * chunks
    ff = w_gate.shape[2]
    own_rows = thinker_keys.shape[0]
    rows = experts * own_rows
    pitch = rows + 16
    place = jnp.stack([lax.axis_index("seq"), lax.axis_index("exp")]).astype(jnp.int32)
    ids, gates = expert_ids.T, gate_values.T

    packed = pl.pallas_call(
        pack_kernel,
        out_shape=jax.ShapeDtypeStruct((experts, 5, own_rows // 2, LANES), BF16),
        in_specs=[SMEM, HBM, HBM],
        out_specs=vmem(1)[0],
        scratch_shapes=[
            pltpu.VMEM(thinker_keys.shape, BF16),
            pltpu.VMEM(thinker_values.shape, BF16),
            pltpu.SemaphoreType.DMA((2,)),
        ],
        compiler_params=params(58),
        name="pack",
    )(thinker_lengths, thinker_keys, thinker_values)
    kv_rows = exchange(packed)

    slot_table, send_cot = pl.pallas_call(
        functools.partial(dispatch_kernel, experts=experts, capacity=capacity),
        out_shape=(
            jax.ShapeDtypeStruct((2 * top, tokens), jnp.int32),
            jax.ShapeDtypeStruct((slots * chunks, LANES), BF16),
        ),
        in_specs=vmem(3),
        out_specs=tuple(vmem(2)),
        compiler_params=params(24),
        name="dispatch",
    )(ids, gates, cotangent)

    segment = pl.pallas_call(
        segment_kernel,
        out_shape=jax.ShapeDtypeStruct((pitch, 2 * LANES), BF16),
        in_specs=vmem(1),
        out_specs=vmem(1)[0],
        compiler_params=params(16),
        name="segment",
    )(kv_rows)
    lower = jnp.concatenate(
        [w_down[0][i * LANES : (i + 1) * LANES, :] for i in range(ff // LANES)], axis=1
    )
    shard = jnp.concatenate([w_gate[0], w_up[0], lower], axis=0)
    segment, send_cot, shard = lax.optimization_barrier((segment, send_cot, shard))
    kv_all = lax.all_gather(segment, "seq", axis=0, tiled=True)
    recv_cot = exchange(send_cot.reshape(experts, each, LANES))
    weights = lax.all_gather(shard, "seq", axis=0, tiled=False)

    send_rows = attend(
        place,
        thinker_lengths,
        kv_all.reshape(shards, pitch, 2 * LANES),
        queries,
        hidden,
        out_proj,
        slot_table,
        rows=rows,
        slots=slots,
    )
    send_rows, recv_cot = lax.optimization_barrier((send_rows, recv_cot))
    recv_rows = exchange(send_rows.reshape(experts, each, LANES))
    down_back = pl.pallas_call(
        prepare_kernel,
        out_shape=jax.ShapeDtypeStruct((slots, ff), F32),
        in_specs=[vmem(1)[0], HBM],
        out_specs=vmem(1)[0],
        scratch_shapes=[
            pltpu.VMEM((slots, width), BF16),
            pltpu.VMEM((shards, LANES, ff), BF16),
            pltpu.SemaphoreType.DMA((shards,)),
        ],
        compiler_params=params(50),
        cost_estimate=pl.CostEstimate(
            flops=40 * slots * width * ff, bytes_accessed=0, transcendentals=0
        ),
        name="prepare",
    )(recv_cot.reshape(slots * chunks, LANES), weights)
    back = expert(
        recv_rows.reshape(slots * chunks, LANES), weights, down_back, capacity=capacity
    )
    home = exchange(back)

    grad_input, grad_gates = pl.pallas_call(
        functools.partial(combine_kernel, capacity=capacity),
        out_shape=(
            jax.ShapeDtypeStruct((tokens, width), F32),
            jax.ShapeDtypeStruct((top, tokens), BF16),
        ),
        in_specs=vmem(5),
        out_specs=tuple(vmem(2)),
        scratch_shapes=[pltpu.VMEM((slots, width), BF16)],
        compiler_params=params(24),
        name="combine",
    )(home, home[:, each, :], ids, gates, slot_table)
    return grad_input, grad_gates.T


def solution(mesh):
    both = P(("seq", "exp"), None)
    return jax.shard_map(
        local,
        mesh=mesh,
        in_specs=(
            both,
            both,
            both,
            both,
            P(("seq", "exp")),
            P(),
            both,
            both,
            P("exp", "seq", None),
            P("exp", "seq", None),
            P("exp", None, "seq"),
            both,
        ),
        out_specs=(both, both),
        check_vma=False,
    )
```
